32 devices in a mesh: dp: 8 (over z, core), mp: 4 (over y, x).
Axes of the slice: x: 2, y: 2, z: 4, core: 2. Of those that a mesh axis runs over, the one named last changes fastest.
Arguments:
- tokens: bfloat16 [4096, 1280], P('dp'), may hold values from -6 to 6
- norm_gain: float32 [1280], replicated, may hold values from 0.25 to 1.75
- widen_weight: bfloat16 [1280, 5120], P(None, 'mp'), may hold values from -0.15625 to 0.15625
- narrow_weight: bfloat16 [5120, 1280], P('mp'), may hold values from -0.078125 to 0.078125
- final_gain: float32 [1280], replicated, may hold values from 0.25 to 1.75
- adaptor_in: bfloat16 [3, 1280, 1280], P(None, None, 'mp'), may hold values from -0.15625 to 0.15625
- head_dino: bfloat16 [1280, 1536], P('mp'), may hold values from -0.15625 to 0.15625
- head_siglip: bfloat16 [1280, 1152], P('mp'), may hold values from -0.15625 to 0.15625
- head_sam: bfloat16 [1280, 1280], P('mp'), may hold values from -0.15625 to 0.15625
- teacher_dino: bfloat16 [2, 4096, 1536], P(None, 'dp', 'mp'), may hold values from -6 to 6
- teacher_siglip: bfloat16 [2, 4096, 1152], P(None, 'dp', 'mp'), may hold values from -6 to 6
- teacher_sam: bfloat16 [2, 4096, 1280], P(None, 'dp', 'mp'), may hold values from -6 to 6
- step_lags: int32 [3], replicated, may hold values from 1 to 2, as said below
- owner_slot: int32 [128], replicated, may hold values from 0 to 127, as said below
Outputs:
- grad_widen: float32 [5120, 1280], P('mp', 'dp')
- grad_narrow: float32 [5120, 1280], P('mp', 'dp')
- grad_adaptor: float32 [3, 1280, 1280], P(None, 'dp', 'mp')
- grad_dino: float32 [1280, 1536], P('mp', 'dp')
- grad_siglip: float32 [1280, 1152], P('mp', 'dp')
- grad_sam: float32 [1280, 1280], P('mp', 'dp')
The draws below stay inside these ranges and needn't reach their ends.
Inputs may be any that keep to these rules, and one draw needn't show every extreme that they name: owner_slot is a permutation; of the 16 images in each aligned block of 16 images, exactly 2 have slots in each aligned block of 16 slots. `step_lags`: the three lags are not all equal.
All inputs are finite; a program needn't handle non-finite values.
Results may differ from the reference program's by a relative error of at most 0.02.
Values may be sent and summed in bfloat16 or wider, within the bound.
No kernel may reach another device: no remote copies, remote signals or barrier semaphores. Data moves between devices by JAX's collectives and lax.ppermute only.
A program may use at most 128 MiB of HBM per device.

```python
import jax
import jax.numpy as jnp
from jax import lax

D = 1280
FF = 5120
HID = 1280
C_DINO = 1536
C_SIGLIP = 1152
C_SAM = 1280
PATCH = 32
IMG_DP = 16
IMAGES = 128
TOKENS = 4096


def draw_owner_slot(key, part):
    groups = IMAGES // IMG_DP
    share = IMG_DP // groups
    key_images, key_slots = jax.random.split(jax.random.fold_in(key, 7))
    image_perm = jax.vmap(lambda sub: jax.random.permutation(sub, IMG_DP))(jax.random.split(key_images, groups))
    slot_perm = jax.vmap(lambda sub: jax.random.permutation(sub, IMG_DP))(jax.random.split(key_slots, groups))
    source = jnp.arange(groups, dtype=jnp.int32)[:, None, None]
    target = jnp.arange(groups, dtype=jnp.int32)[None, :, None]
    within = jnp.arange(share, dtype=jnp.int32)[None, None, :]
    image = source * IMG_DP + image_perm[source, target * share + within]
    slot = target * IMG_DP + slot_perm[target, source * share + within]
    return jnp.zeros((IMAGES,), jnp.int32).at[image.reshape(-1)].set(slot.reshape(-1).astype(jnp.int32))


def draw_step_lags(key, part):
    key_free, key_order = jax.random.split(jax.random.fold_in(key, 11))
    free = jax.random.randint(key_free, (1,), 1, 3, dtype=jnp.int32)
    values = jnp.concatenate([jnp.array([1, 2], dtype=jnp.int32), free.astype(jnp.int32)])
    return jax.random.permutation(key_order, values).astype(jnp.int32)


def spiked(drawn, stream_key, source, target, shards_of, factor):
    owner, partner = [(jnp.arange(drawn.shape[position]) // (drawn.shape[position] // shards_of)).reshape([-1 if axis == position else 1 for axis in range(drawn.ndim)]) for position in (source, target)]
    chosen = jax.random.permutation(stream_key, shards_of)[partner]
    strong = (owner == chosen) | (owner == (partner + shards_of // 2) % shards_of)
    return jnp.where(strong, factor * drawn, drawn)


def steps_of(key, extent, pieces, low, high):
    level, own = 1.0, jax.random.fold_in(key, 6)
    for dim, blocks in pieces:
        draws = jnp.exp(jax.random.uniform(jax.random.fold_in(own, dim), (blocks,), jnp.float32, low / len(pieces), high / len(pieces)))
        level = level * jnp.repeat(draws, extent[dim] // blocks).reshape([-1 if axis == dim else 1 for axis in range(len(extent))])
    return level


def gaussian(key, shape, deviation, reach, cuts=(), kind=jnp.bfloat16):
    values = deviation * jax.random.normal(key, shape, jnp.float32)
    if cuts:
        values = values * steps_of(key, shape, cuts, -0.22, 0.18)
    return jnp.clip(values, -reach, reach).astype(kind)


def heavy_noise(stream_key, shape, scale, bound, shards, heavy, kind=jnp.bfloat16):
    entries = scale * jax.random.normal(stream_key, shape, jnp.float32)
    if shards:
        entries = entries * steps_of(stream_key, shape, shards, -0.22, 0.18)
    return jnp.clip(spiked(entries, jax.random.fold_in(stream_key, 3), *heavy), -bound, bound).astype(kind)


def setup_inputs(seed: int = 0) -> dict:
    keys = jax.random.split(jax.random.key(seed), 15)
    tokens = heavy_noise(keys[0], (TOKENS, D), 1.0, 6.0, ((0, 8),), (0, 1, 8, 2.0))
    norm_gain = jnp.clip(1.0 + 0.15 * jax.random.normal(keys[1], (D,), jnp.float32), 0.25, 1.75)
    widen_weight = gaussian(keys[2], (D, FF), D ** -0.5, 0.15625, ((1, 4),))
    narrow_weight = gaussian(keys[3], (FF, D), FF ** -0.5, 0.078125, ((0, 4),))
    final_gain = jnp.clip(1.0 + 0.15 * jax.random.normal(keys[4], (D,), jnp.float32), 0.25, 1.75)
    adaptor_in = gaussian(keys[5], (3, D, HID), D ** -0.5, 0.15625, ((2, 4),))
    head_dino = gaussian(keys[6], (HID, C_DINO), HID ** -0.5, 0.15625, ((0, 4),))
    head_siglip = gaussian(keys[7], (HID, C_SIGLIP), HID ** -0.5, 0.15625, ((0, 4),))
    head_sam = gaussian(keys[8], (HID, C_SAM), HID ** -0.5, 0.15625, ((0, 4),))
    teacher_dino = gaussian(keys[9], (2, TOKENS, C_DINO), 1.0, 6.0, ((1, 8), (2, 4)))
    teacher_siglip = gaussian(keys[10], (2, TOKENS, C_SIGLIP), 1.0, 6.0, ((1, 8), (2, 4)))
    teacher_sam = gaussian(keys[11], (2, TOKENS, C_SAM), 1.0, 6.0, ((1, 8), (2, 4)))
    step_lags = draw_step_lags(jax.random.fold_in(keys[14], 71), 0)
    owner_slot = draw_owner_slot(jax.random.fold_in(keys[14], 71), 0)
    return {"tokens": tokens, "norm_gain": norm_gain, "widen_weight": widen_weight, "narrow_weight": narrow_weight, "final_gain": final_gain, "adaptor_in": adaptor_in, "head_dino": head_dino, "head_siglip": head_siglip, "head_sam": head_sam, "teacher_dino": teacher_dino, "teacher_siglip": teacher_siglip, "teacher_sam": teacher_sam, "step_lags": step_lags, "owner_slot": owner_slot}


slope_coef = 0.7978845608028654
cubic_coef = 0.044715

def smooth(value):
    return 0.5 * value * (1.0 + jnp.tanh(slope_coef * (value + cubic_coef * value * value * value)))

def smooth_slope(value):
    tangent = jnp.tanh(slope_coef * (value + cubic_coef * value * value * value))
    return 0.5 * (1.0 + tangent) + 0.5 * value * (1.0 - tangent * tangent) * slope_coef * (1.0 + 3.0 * cubic_coef * value * value)

def normalize(value, gain):
    centre = value - lax.optimization_barrier(jnp.mean(value, axis=-1, keepdims=True))
    inverse = lax.rsqrt(lax.optimization_barrier(jnp.mean(centre * centre, axis=-1, keepdims=True)) + 1e-06)
    normal = centre * inverse
    return (normal * gain, normal, inverse)

def normalize_back(upstream, gain, normal, inverse):
    scaled = upstream * gain
    return inverse * (scaled - lax.optimization_barrier(jnp.mean(scaled, axis=-1, keepdims=True)) - normal * lax.optimization_barrier(jnp.mean(scaled * normal, axis=-1, keepdims=True)))

def finish(product, square_student, square_target, student, target):
    joint = lax.rsqrt(square_student * square_target)
    cosine = product * joint
    slope = cosine[:, None] * student / square_student[:, None] - target * joint[:, None]
    return (cosine, slope)

def reference(tokens, norm_gain, widen_weight, narrow_weight, final_gain, adaptor_in, head_dino, head_siglip, head_sam, teacher_dino, teacher_siglip, teacher_sam, step_lags, owner_slot):
    heads = (head_dino, head_siglip, head_sam)
    teachers = (teacher_dino, teacher_siglip, teacher_sam)
    placing = jnp.argsort(owner_slot).astype(jnp.int32)
    first, normal_one, inverse_one = normalize(tokens.astype(jnp.float32), norm_gain)
    first = first.astype(jnp.bfloat16)
    widened = jnp.dot(first, widen_weight, preferred_element_type=jnp.float32)
    active = smooth(widened).astype(jnp.bfloat16)
    hidden = tokens.astype(jnp.float32) + jnp.dot(active, narrow_weight, preferred_element_type=jnp.float32)
    final, normal_two, inverse_two = normalize(hidden, final_gain)
    final = final.astype(jnp.bfloat16)
    upstream = jnp.zeros(hidden.shape, jnp.float32)
    head_grads = []
    adaptor_grads = []
    for index in range(3):
        before = jnp.dot(final, adaptor_in[index], preferred_element_type=jnp.float32)
        lifted = smooth(before).astype(jnp.bfloat16)
        student = jnp.dot(lifted, heads[index], preferred_element_type=jnp.float32)
        stale = lax.dynamic_index_in_dim(teachers[index], step_lags[index] - 1, 0, keepdims=False)
        width = stale.shape[-1]
        target = jnp.take(stale.reshape(IMAGES, PATCH, width), placing, axis=0).reshape(TOKENS, width).astype(jnp.float32)
        product = lax.optimization_barrier(jnp.sum(student * target, axis=-1))
        square_student = lax.optimization_barrier(jnp.sum(student * student, axis=-1)) + 1e-06
        square_target = lax.optimization_barrier(jnp.sum(target * target, axis=-1)) + 1e-06
        cosine, slope = finish(product, square_student, square_target, student, target)
        slope = slope.astype(jnp.bfloat16)
        head_grads.append(jnp.dot(lifted.T, slope, preferred_element_type=jnp.float32))
        back = jnp.dot(slope, heads[index].T, preferred_element_type=jnp.float32)
        inner = (back * smooth_slope(before)).astype(jnp.bfloat16)
        adaptor_grads.append(jnp.dot(final.T, inner, preferred_element_type=jnp.float32))
        upstream = upstream + jnp.dot(inner, adaptor_in[index].T, preferred_element_type=jnp.float32)
    through = normalize_back(upstream, final_gain, normal_two, inverse_two).astype(jnp.bfloat16)
    grad_narrow = jnp.dot(active.T, through, preferred_element_type=jnp.float32)
    back_two = jnp.dot(through, narrow_weight.T, preferred_element_type=jnp.float32)
    inner_two = (back_two * smooth_slope(widened)).astype(jnp.bfloat16)
    grad_widen = jnp.dot(inner_two.T, first, preferred_element_type=jnp.float32)
    return (grad_widen, grad_narrow, jnp.stack(adaptor_grads), head_grads[0], head_grads[1], head_grads[2])
```

```python
import jax
import jax.numpy as jnp
from jax import lax
from jax.sharding import PartitionSpec as P

PATCH = 32


slope_coef = 0.7978845608028654
cubic_coef = 0.044715


def smooth(value):
    return 0.5 * value * (1.0 + jnp.tanh(slope_coef * (value + cubic_coef * value * value * value)))


def smooth_slope(value):
    tangent = jnp.tanh(slope_coef * (value + cubic_coef * value * value * value))
    return 0.5 * (1.0 + tangent) + 0.5 * value * (1.0 - tangent * tangent) * slope_coef * (
        1.0 + 3.0 * cubic_coef * value * value
    )


def normalize(value, gain):
    centre = value - jnp.mean(value, axis=-1, keepdims=True)
    inverse = lax.rsqrt(jnp.mean(centre * centre, axis=-1, keepdims=True) + 1e-06)
    normal = centre * inverse
    return (normal * gain, normal, inverse)


def normalize_back(upstream, gain, normal, inverse):
    scaled = upstream * gain
    return inverse * (
        scaled
        - jnp.mean(scaled, axis=-1, keepdims=True)
        - normal * jnp.mean(scaled * normal, axis=-1, keepdims=True)
    )


def finish(product, square_student, square_target, student, target):
    joint = lax.rsqrt(square_student * square_target)
    cosine = product * joint
    slope = cosine[:, None] * student / square_student[:, None] - target * joint[:, None]
    return (cosine, slope)


def swap(value, axis, offset):
    count = lax.axis_size(axis)
    return lax.ppermute(value, axis, [(i, i ^ offset) for i in range(count)])


def ordered(value, count, position):
    cut = value.reshape((count, value.shape[0] // count) + value.shape[1:])
    return [
        lax.dynamic_index_in_dim(cut, position ^ j, 0, keepdims=False) for j in range(count)
    ]


def scatter_sum(blocks, axis):
    total = blocks[0]
    arrived = [
        swap(blocks[j].astype(jnp.bfloat16), axis, j) for j in range(1, len(blocks))
    ]
    for piece in arrived:
        total = total + piece.astype(jnp.float32)
    return total


def gather(piece, axis):
    return jnp.concatenate(
        [piece] + [swap(piece, axis, j) for j in range(1, lax.axis_size(axis))], axis=0
    )


def reduce_over_images(value, groups, group):
    cut = value.reshape(groups // 2, 2, value.shape[0] // groups, value.shape[1])
    side = group % 2
    theirs = lax.dynamic_index_in_dim(cut, 1 - side, 1, keepdims=False)
    mine = lax.dynamic_index_in_dim(cut, side, 1, keepdims=False)
    paired = mine.astype(jnp.float32) + swap(theirs.astype(jnp.bfloat16), "dp", 1).astype(
        jnp.float32
    )
    pair = group // 2
    total = lax.dynamic_index_in_dim(paired, pair, 0, keepdims=False)
    sending = paired.astype(jnp.bfloat16)
    arrived = [
        swap(lax.dynamic_index_in_dim(sending, pair ^ o, 0, keepdims=False), "dp", 2 * o)
        for o in range(1, groups // 2)
    ]
    for piece in arrived:
        total = total + piece.astype(jnp.float32)
    return total


def one_hot_rows(place, images):
    rows = images * PATCH
    to = lax.broadcasted_iota(jnp.int32, (rows, rows), 0)
    spread = jnp.broadcast_to(place[:, None], (images, PATCH)).reshape(1, rows) * PATCH
    inner = lax.broadcasted_iota(jnp.int32, (rows, rows), 1) % PATCH
    return (to == spread + inner).astype(jnp.bfloat16)


def local(
    tokens,
    norm_gain,
    widen_weight,
    narrow_weight,
    final_gain,
    adaptor_in,
    head_dino,
    head_siglip,
    head_sam,
    teacher_dino,
    teacher_siglip,
    teacher_sam,
    step_lags,
    owner_slot,
):
    groups = lax.axis_size("dp")
    members = lax.axis_size("mp")
    group = lax.axis_index("dp")
    member = lax.axis_index("mp")
    rows = tokens.shape[0]
    images = rows // PATCH
    share = images // groups
    block = rows // members
    heads = (head_dino, head_siglip, head_sam)
    teachers = (teacher_dino, teacher_siglip, teacher_sam)
    widths = [teacher.shape[-1] for teacher in teachers]
    exact = dict(preferred_element_type=jnp.float32)

    slots = owner_slot.reshape(groups, images)
    rank = jnp.sum(slots[:, :, None] > slots[:, None, :], axis=2, dtype=jnp.int32) % share
    source = lax.broadcasted_iota(jnp.int32, (groups, images), 0)
    leaving = (slots // images ^ group) * share + rank
    leaving = lax.dynamic_index_in_dim(leaving, group, 0, keepdims=False)
    landing = (source ^ group) * share + rank
    slot_rows = group * images + lax.broadcasted_iota(jnp.int32, (images,), 0)
    found = slots.reshape(1, -1) == slot_rows[:, None]
    landed = jnp.sum(jnp.where(found, landing.reshape(1, -1), 0), axis=1)
    position = lax.broadcasted_iota(jnp.int32, (images,), 0) ^ (member * (images // members))
    at = lax.broadcasted_iota(jnp.int32, (images, images), 0)
    place = jnp.sum(jnp.where(landed[None, :] == at, position[None, :], 0), axis=1)

    stale = jnp.concatenate(
        [
            lax.dynamic_index_in_dim(teacher, step_lags[index] - 1, 0, keepdims=False)
            for index, teacher in enumerate(teachers)
        ],
        axis=-1,
    )
    packed = jnp.dot(one_hot_rows(leaving, images), stale, **exact).astype(jnp.bfloat16)
    packed = packed.reshape(groups // 2, 2, share * PATCH, -1)
    crossed = swap(packed[:, 1], "dp", 1)
    pairs = jnp.stack([packed[:, 0], crossed], axis=1)
    arrived = jnp.stack(
        [pairs[0]] + [swap(pairs[o], "dp", 2 * o) for o in range(1, groups // 2)]
    ).reshape(rows, -1)
    owned = jnp.dot(one_hot_rows(place, images), arrived, **exact).astype(jnp.bfloat16)

    tokens = jnp.concatenate(ordered(tokens, members, member), axis=0)
    first, _, _ = normalize(tokens.astype(jnp.float32), norm_gain)
    first = first.astype(jnp.bfloat16)
    widened = jnp.dot(first, widen_weight, **exact)
    active = smooth(widened).astype(jnp.bfloat16)
    mixed = jnp.dot(active, narrow_weight, **exact).reshape(members, block, -1)
    hidden = tokens[:block].astype(jnp.float32) + scatter_sum(list(mixed), "mp")
    final_rows, normal_rows, inverse_rows = normalize(hidden, final_gain)
    final = gather(final_rows.astype(jnp.bfloat16), "mp")

    owned = owned.reshape(members, block, -1)
    parts = jnp.stack([owned[0]] + [swap(owned[j], "mp", j) for j in range(1, members)])
    parts = [
        lax.dynamic_index_in_dim(parts, member ^ j, 0, keepdims=False) for j in range(members)
    ]

    befores, lifteds, students = [], [], []
    for index in range(3):
        before = jnp.dot(final, adaptor_in[index], **exact)
        lifted = smooth(before).astype(jnp.bfloat16)
        partial = jnp.dot(lifted, heads[index], **exact).reshape(members, block, -1)
        befores.append(before)
        lifteds.append(lifted)
        students.append(scatter_sum(list(partial), "mp"))
    slopes = []
    start = 0
    for index in range(3):
        student = students[index]
        target = jnp.concatenate(
            [part[:, start : start + widths[index]] for part in parts], axis=-1
        ).astype(jnp.float32)
        start += widths[index]
        product = jnp.sum(student * target, axis=-1)
        square_student = jnp.sum(student * student, axis=-1) + 1e-06
        square_target = jnp.sum(target * target, axis=-1) + 1e-06
        _, slope = finish(product, square_student, square_target, student, target)
        slopes.append(gather(slope.astype(jnp.bfloat16), "mp"))
    inners = []
    upstream = 0.0
    for index in range(3):
        back = jnp.einsum("rc,hc->rh", slopes[index], heads[index], **exact)
        inner = (back * smooth_slope(befores[index])).astype(jnp.bfloat16)
        inners.append(inner)
        upstream = upstream + jnp.einsum("rh,dh->rd", inner, adaptor_in[index], **exact)
    upstream = scatter_sum(list(upstream.reshape(members, block, -1)), "mp")
    through_rows = normalize_back(upstream, final_gain, normal_rows, inverse_rows)
    through = gather(through_rows.astype(jnp.bfloat16), "mp")

    head_grads = [
        reduce_over_images(
            jnp.einsum("rc,rh->ch", slopes[index], lifteds[index], **exact), groups, group
        ).T
        for index in range(3)
    ]
    grad_adaptor = jnp.concatenate(
        [jnp.einsum("rd,rh->dh", final, inner, **exact) for inner in inners], axis=-1
    )
    grad_adaptor = reduce_over_images(grad_adaptor, groups, group)
    grad_adaptor = jnp.stack(jnp.split(grad_adaptor, 3, axis=-1))

    grad_narrow = jnp.einsum("rd,rf->df", through, active, **exact)
    grad_narrow = reduce_over_images(grad_narrow, groups, group).T
    back_two = jnp.einsum("rd,fd->rf", through, narrow_weight, **exact)
    inner_two = (back_two * smooth_slope(widened)).astype(jnp.bfloat16)
    grad_widen = jnp.einsum("rd,rf->df", first, inner_two, **exact)
    grad_widen = reduce_over_images(grad_widen, groups, group).T
    return (grad_widen, grad_narrow, grad_adaptor, *head_grads)


def solution(mesh):
    placed = (
        P("dp", None),
        P(),
        P(None, "mp"),
        P("mp", None),
        P(),
        P(None, None, "mp"),
        P("mp", None),
        P("mp", None),
        P("mp", None),
        P(None, "dp", "mp"),
        P(None, "dp", "mp"),
        P(None, "dp", "mp"),
        P(),
        P(),
    )
    return jax.shard_map(
        local,
        mesh=mesh,
        in_specs=placed,
        out_specs=(
            P("mp", "dp"),
            P("mp", "dp"),
            P(None, "dp", "mp"),
            P("mp", "dp"),
            P("mp", "dp"),
            P("mp", "dp"),
        ),
        check_vma=False,
    )
```

```python
import functools

import jax
import jax.numpy as jnp
from jax import lax
from jax.experimental import pallas as pl
from jax.experimental.pallas import tpu as pltpu
from jax.sharding import PartitionSpec as P

PATCH = 32


slope_coef = 0.7978845608028654
cubic_coef = 0.044715


def smooth(value):
    return 0.5 * value * (1.0 + jnp.tanh(slope_coef * (value + cubic_coef * value * value * value)))


def smooth_slope(value):
    tangent = jnp.tanh(slope_coef * (value + cubic_coef * value * value * value))
    return 0.5 * (1.0 + tangent) + 0.5 * value * (1.0 - tangent * tangent) * slope_coef * (
        1.0 + 3.0 * cubic_coef * value * value
    )


def normalize(value, gain):
    centre = value - jnp.mean(value, axis=-1, keepdims=True)
    inverse = lax.rsqrt(jnp.mean(centre * centre, axis=-1, keepdims=True) + 1e-06)
    normal = centre * inverse
    return (normal * gain, normal, inverse)


def normalize_back(upstream, gain, normal, inverse):
    scaled = upstream * gain
    return inverse * (
        scaled
        - jnp.mean(scaled, axis=-1, keepdims=True)
        - normal * jnp.mean(scaled * normal, axis=-1, keepdims=True)
    )


def finish(product, square_student, square_target, student, target):
    joint = lax.rsqrt(square_student * square_target)
    cosine = product * joint
    slope = cosine[:, None] * student / square_student[:, None] - target * joint[:, None]
    return (cosine, slope)


def swap(value, axis, offset):
    count = lax.axis_size(axis)
    return lax.ppermute(value, axis, [(i, i ^ offset) for i in range(count)])


def ordered(value, count, position):
    cut = value.reshape((count, value.shape[0] // count) + value.shape[1:])
    return [
        lax.dynamic_index_in_dim(cut, position ^ j, 0, keepdims=False) for j in range(count)
    ]


def scatter_sum(blocks, axis):
    total = blocks[0]
    arrived = [
        swap(blocks[j].astype(jnp.bfloat16), axis, j) for j in range(1, len(blocks))
    ]
    for piece in arrived:
        total = total + piece.astype(jnp.float32)
    return total


def gather(piece, axis):
    return jnp.concatenate(
        [piece] + [swap(piece, axis, j) for j in range(1, lax.axis_size(axis))], axis=0
    )


def bits_of(count, low_first):
    bits = [1 << k for k in range(count.bit_length() - 1)]
    return bits if low_first else bits[::-1]


def scatter_halving(blocks, axis, low_first):
    held = dict(enumerate(blocks))
    size = blocks[0].shape[0]
    bits = bits_of(len(blocks), low_first)
    for bit in bits:
        leaving = [j for j in sorted(held) if j & bit]
        packed = jnp.concatenate([held.pop(j).astype(jnp.bfloat16) for j in leaving], axis=0)
        packed = swap(packed, axis, bit)
        if bit == bits[-1]:
            return held[0], packed
        for k, j in enumerate(leaving):
            held[j ^ bit] = held[j ^ bit] + packed[k * size : (k + 1) * size].astype(jnp.float32)


def gather_doubling(piece, axis, low_first):
    held = {0: piece}
    size = piece.shape[0]
    for bit in bits_of(lax.axis_size(axis), low_first):
        order = sorted(held)
        packed = held[0] if len(order) == 1 else jnp.concatenate([held[j] for j in order], axis=0)
        packed = swap(packed, axis, bit)
        for k, j in enumerate(order):
            held[j ^ bit] = packed[k * size : (k + 1) * size]
    return jnp.concatenate([held[j] for j in sorted(held)], axis=0)


def reverse_bits(value, count):
    result = 0
    for k in range(count.bit_length() - 1):
        result = result * 2 + (value >> k) % 2
    return result


def limits(flops=0, moved=0):
    return dict(
        compiler_params=pltpu.CompilerParams(vmem_limit_bytes=48 * 2**20),
        cost_estimate=pl.CostEstimate(flops=flops, bytes_accessed=moved, transcendentals=0),
    )


IN_VMEM = pl.BlockSpec(memory_space=pltpu.VMEM)
IN_SMEM = pl.BlockSpec(memory_space=pltpu.SMEM)
IN_PLACE = pl.BlockSpec(memory_space=pl.ANY)


def pack_kernel(groups, images, turned, lag_ref, slot_ref, group_ref, *refs):
    count = len(turned)
    teachers, (keep_ref, send_ref) = refs[:count], refs[count : count + 2]
    held, sems = refs[count + 2 : -1], refs[-1]
    share = images // groups
    group = group_ref[0]
    copies = [
        pltpu.make_async_copy(teachers[t].at[lag_ref[t] - 1], held[t], sems.at[t])
        for t in range(count)
    ]
    for copy in copies:
        copy.start()
    slots = [slot_ref[group * images + i] for i in range(images)]
    places = []
    for i in range(images):
        rank = sum((slots[j] < slots[i]).astype(jnp.int32) for j in range(images) if j != i)
        away = lax.div(slots[i], images) ^ group
        spot = (away >> 1) * share + lax.rem(rank, share)
        places.append((away & 1, pl.ds(pl.multiple_of(spot * PATCH, PATCH), PATCH)))
    start = 0
    for t in range(count):
        copies[t].wait()
        value = held[t][...]
        if turned[t]:
            value = value.T
        columns = slice(start, start + value.shape[1])
        start += value.shape[1]
        for i, (side, to) in enumerate(places):
            piece = value[i * PATCH : (i + 1) * PATCH, :]

            @pl.when(side == 0)
            def _(piece=piece, to=to, columns=columns):
                keep_ref[to, columns] = piece

            @pl.when(side != 0)
            def _(piece=piece, to=to, columns=columns):
                send_ref[to, columns] = piece


def pack(step_lags, owner_slot, group, teachers, groups, images):
    rows = images * PATCH
    width = sum(teacher.shape[-1] for teacher in teachers)
    turned = [teacher.shape[-1] % 128 != 0 for teacher in teachers]
    teachers = [
        jnp.swapaxes(teacher, 1, 2) if turn else teacher for teacher, turn in zip(teachers, turned)
    ]
    half = jax.ShapeDtypeStruct((rows // 2, width), jnp.bfloat16)
    return pl.pallas_call(
        functools.partial(pack_kernel, groups, images, turned),
        out_shape=(half, half),
        in_specs=[IN_SMEM] * 3 + [IN_PLACE] * len(teachers),
        out_specs=(IN_VMEM, IN_VMEM),
        scratch_shapes=[pltpu.VMEM(teacher.shape[1:], jnp.bfloat16) for teacher in teachers]
        + [pltpu.SemaphoreType.DMA((len(teachers),))],
        name="pack",
        **limits(moved=4 * rows * width),
    )(step_lags, owner_slot, group.reshape(1), *teachers)


def place_kernel(images, place_ref, *refs):
    out_ref = refs[-1]
    each = images // (len(refs) - 1)
    for a in range(images):
        to = pl.ds(pl.multiple_of(place_ref[a] * PATCH, PATCH), PATCH)
        k = a % each
        out_ref[to, :] = refs[a // each][k * PATCH : (k + 1) * PATCH, :]


def loss_kernel(start, width, count, member_ref, *refs):
    parts, terms = refs[:count], refs[count:]
    sides = len(terms) // 3
    terms, slope_refs = terms[: 2 * sides], terms[2 * sides :]
    member = member_ref[0]
    pieces = [part[:, start : start + width].astype(jnp.float32) for part in parts]
    for bit in bits_of(count, True):
        flipped = (member & bit) != 0
        pieces = [jnp.where(flipped, pieces[j ^ bit], pieces[j]) for j in range(count)]
    target = jnp.concatenate(pieces, axis=-1)
    student = [
        terms[2 * k][...] + terms[2 * k + 1][...].astype(jnp.float32) for k in range(sides)
    ]
    student = student[0] if sides == 1 else jnp.concatenate(student, axis=-1)
    product = jnp.sum(student * target, axis=-1, keepdims=True)
    square_student = jnp.sum(student * student, axis=-1, keepdims=True) + 1e-06
    square_target = jnp.sum(target * target, axis=-1, keepdims=True) + 1e-06
    joint = lax.rsqrt(square_student * square_target)
    cosine = product * joint
    slope = ((cosine / square_student) * student - target * joint).astype(jnp.bfloat16)
    wide = slope.shape[1] // sides
    for k in range(sides):
        slope_refs[k][...] = slope[:, k * wide : (k + 1) * wide]


def loss(member, terms, parts, start, width):
    flat = [value for pair in terms for value in pair]
    return pl.pallas_call(
        functools.partial(loss_kernel, start, width, len(parts)),
        out_shape=[jax.ShapeDtypeStruct(last.shape, jnp.bfloat16) for _, last in terms],
        in_specs=[IN_SMEM] + [IN_VMEM] * (len(parts) + len(flat)),
        out_specs=[IN_VMEM] * len(terms),
        name="loss",
        **limits(moved=10 * sum(last.size for _, last in terms)),
    )(member.reshape(1), *parts, *flat)


def beside(refs):
    return refs[0][...] if len(refs) == 1 else jnp.concatenate([r[...] for r in refs], axis=1)


def product_kernel(groups, shape, spot_ref, *refs):
    keep_ref, send_ref = refs[-2:]
    side, base = spot_ref[0] != 0, spot_ref[1]
    tall = keep_ref.shape[1]
    used = column = 0
    for lefts, rights in shape:
        left = beside(refs[used : used + lefts])
        right = beside(refs[used + lefts : used + lefts + rights])
        used += lefts + rights
        cut, wide = left.shape[1] // groups, right.shape[1]
        columns = slice(column, column + wide)
        column += wide
        full = lax.dot_general(
            left, right, (((0,), (0,)), ((), ())), preferred_element_type=jnp.float32
        )
        for pair in range(groups // 2):
            even = full[2 * pair * cut : (2 * pair + 1) * cut, :]
            odd = full[(2 * pair + 1) * cut : (2 * pair + 2) * cut, :]
            at = base ^ reverse_bits(pair, groups // 2)
            keep_ref[at, :cut, columns] = jnp.where(side, odd, even).astype(jnp.bfloat16)
            send_ref[at, :cut, columns] = jnp.where(side, even, odd).astype(jnp.bfloat16)
            if cut < tall:
                rest = jnp.zeros((tall - cut, wide), jnp.bfloat16)
                keep_ref[at, cut:, columns] = rest
                send_ref[at, cut:, columns] = rest


def product(pairs, groups, group):
    talls = [sum(left.shape[1] for left in lefts) for lefts, _ in pairs]
    wides = [sum(right.shape[1] for right in rights) for _, rights in pairs]
    tall, wide = max(talls) // groups, sum(wides)
    half = jax.ShapeDtypeStruct((groups // 2, tall, wide), jnp.bfloat16)
    spot = jnp.stack([group % 2, reverse_bits(group // 2, groups // 2)]).astype(jnp.int32)
    flat = [value for lefts, rights in pairs for value in (*lefts, *rights)]
    return pl.pallas_call(
        functools.partial(product_kernel, groups, [(len(l), len(r)) for l, r in pairs]),
        out_shape=(half, half),
        in_specs=[IN_SMEM] + [IN_VMEM] * len(flat),
        out_specs=(IN_VMEM, IN_VMEM),
        name="product",
        **limits(2 * flat[0].shape[0] * tall * groups * wide, 4 * tall * groups * wide),
    )(spot, *flat)


def pin(*values):
    return lax.optimization_barrier(values)


def begin(halves):
    keep, send = halves
    return (keep, swap(send, "dp", 1), 1)


def advance(state):
    keep, came, bit = state
    if keep.shape[0] == 1:
        return state
    held = keep.astype(jnp.float32) + came.astype(jnp.float32)
    half = held.shape[0] // 2
    return (held[:half], swap(held[half:].astype(jnp.bfloat16), "dp", 2 * bit), 2 * bit)


def complete(state):
    while state[0].shape[0] > 1:
        state = advance(state)
    keep, came, _ = state
    return keep[0].astype(jnp.float32) + came[0].astype(jnp.float32)


def arrive(state, came):
    return (state[0], came, state[2])


def local(
    tokens,
    norm_gain,
    widen_weight,
    narrow_weight,
    final_gain,
    adaptor_in,
    head_dino,
    head_siglip,
    head_sam,
    teacher_dino,
    teacher_siglip,
    teacher_sam,
    step_lags,
    owner_slot,
):
    groups = lax.axis_size("dp")
    members = lax.axis_size("mp")
    group = lax.axis_index("dp")
    member = lax.axis_index("mp")
    rows = tokens.shape[0]
    images = rows // PATCH
    share = images // groups
    block = rows // members
    heads = (head_dino, head_siglip, head_sam)
    teachers = (teacher_dino, teacher_siglip, teacher_sam)
    widths = [teacher.shape[-1] for teacher in teachers]
    exact = dict(preferred_element_type=jnp.float32)

    slots = owner_slot.reshape(groups, images)
    rank = jnp.sum(slots[:, :, None] > slots[:, None, :], axis=2, dtype=jnp.int32) % share
    source = lax.broadcasted_iota(jnp.int32, (groups, images), 0)
    landing = (source ^ group) * share + rank
    slot_rows = group * images + lax.broadcasted_iota(jnp.int32, (images,), 0)
    found = slots.reshape(1, -1) == slot_rows[:, None]
    landed = jnp.sum(jnp.where(found, landing.reshape(1, -1), 0), axis=1)
    position = lax.broadcasted_iota(jnp.int32, (images,), 0) ^ (member * (images // members))
    at = lax.broadcasted_iota(jnp.int32, (images, images), 0)
    place = jnp.sum(jnp.where(landed[None, :] == at, position[None, :], 0), axis=1)

    tokens = jnp.concatenate(ordered(tokens, members, member), axis=0)
    first, _, _ = normalize(tokens.astype(jnp.float32), norm_gain)
    first = lax.optimization_barrier(first.astype(jnp.bfloat16))
    widened = jnp.dot(first, widen_weight, **exact)
    active = smooth(widened).astype(jnp.bfloat16)
    mixed = jnp.dot(active, narrow_weight, **exact).reshape(members, block, -1)
    mixed, step_lags = pin(mixed, step_lags)
    hidden = tokens[:block].astype(jnp.float32) + scatter_sum(list(mixed), "mp")

    kept, crossing = pack(step_lags, owner_slot, group, teachers, groups, images)
    pairs = jnp.stack(
        [
            kept.reshape(groups // 2, share * PATCH, -1),
            swap(crossing, "dp", 1).reshape(groups // 2, share * PATCH, -1),
        ],
        axis=1,
    ).reshape(groups // 2, 2 * share * PATCH, -1)
    arrived = [pairs[0]] + [swap(pairs[o], "dp", 2 * o) for o in range(1, groups // 2)]
    owned = pl.pallas_call(
        functools.partial(place_kernel, images),
        out_shape=jax.ShapeDtypeStruct((rows, sum(widths)), jnp.bfloat16),
        in_specs=[IN_SMEM] + [IN_VMEM] * len(arrived),
        out_specs=IN_VMEM,
        name="place",
        **limits(moved=4 * rows * sum(widths)),
    )(place, *arrived)

    final_rows, normal_rows, inverse_rows = normalize(hidden, final_gain)
    final = gather(final_rows.astype(jnp.bfloat16), "mp")

    owned = owned.reshape(members, block, -1)
    parts = [owned[0]] + [swap(owned[j], "mp", j) for j in range(1, members)]

    ways = ((True, False), (True,), (False,))
    befores, lifteds, students = [], [], []
    for index in range(3):
        before = jnp.dot(final, adaptor_in[index], **exact)
        lifted = smooth(before).astype(jnp.bfloat16)
        partial = jnp.dot(lifted, heads[index], **exact).reshape(members, block, -1)
        befores.append(before)
        lifteds.append(lifted)
        wide = partial.shape[-1] // len(ways[index])
        students.append(
            [
                scatter_halving(list(partial[:, :, k * wide : (k + 1) * wide]), "mp", way)
                for k, way in enumerate(ways[index])
            ]
        )
    slopes = []
    start = 0
    for index in range(3):
        made = loss(member, students[index], parts, start, widths[index])
        start += widths[index]
        slopes.append([gather_doubling(s, "mp", way) for s, way in zip(made, ways[index])])
    inners = []
    upstream = 0.0
    for index in range(3):
        back = 0.0
        wide = slopes[index][0].shape[1]
        for k, slope in enumerate(slopes[index]):
            head = heads[index][:, k * wide : (k + 1) * wide]
            back = back + jnp.einsum("rc,hc->rh", slope, head, **exact)
        inner = (back * smooth_slope(befores[index])).astype(jnp.bfloat16)
        inners.append(inner)
        upstream = upstream + jnp.einsum("rh,dh->rd", inner, adaptor_in[index], **exact)
    upstream = upstream.reshape(members, block, -1)
    came = [swap(upstream[j].astype(jnp.bfloat16), "mp", j) for j in range(1, members)]

    of_heads = begin(product(list(zip(slopes, [[l] for l in lifteds])), groups, group))
    *came, arrived = pin(*came, of_heads[1])
    of_heads = advance(arrive(of_heads, arrived))
    total = upstream[0]
    for piece in came:
        total = total + piece.astype(jnp.float32)
    through_rows = normalize_back(total, final_gain, normal_rows, inverse_rows)
    through_rows = through_rows.astype(jnp.bfloat16)
    came = [swap(through_rows, "mp", j) for j in range(1, members)]
    of_adaptor = begin(product([([final], inners)], groups, group))
    *came, one, two = pin(*came, of_heads[1], of_adaptor[1])
    of_heads = advance(arrive(of_heads, one))
    of_adaptor = advance(arrive(of_adaptor, two))
    through = jnp.concatenate([through_rows, *came], axis=0)

    of_narrow = begin(product([([through], [active])], groups, group))
    back_two = jnp.einsum("rd,fd->rf", through, narrow_weight, **exact)
    inner_two = (back_two * smooth_slope(widened)).astype(jnp.bfloat16)
    inner_two, arrived = pin(inner_two, of_narrow[1])
    of_narrow = advance(arrive(of_narrow, arrived))
    of_widen = begin(product([([first], [inner_two])], groups, group))
    one, two = pin(of_adaptor[1], of_widen[1])
    of_adaptor = advance(arrive(of_adaptor, one))
    of_widen = advance(arrive(of_widen, two))
    one, two = pin(of_narrow[1], of_heads[1])
    of_narrow = advance(arrive(of_narrow, one))
    of_heads = arrive(of_heads, two)
    one, two = pin(of_widen[1], of_adaptor[1])
    of_widen = advance(arrive(of_widen, one))
    of_adaptor = arrive(of_adaptor, two)
    reduced = complete(of_heads)
    wide = lifteds[0].shape[1]
    head_grads = [
        reduced[: heads[k].shape[1] // groups, k * wide : (k + 1) * wide].T for k in range(3)
    ]
    grad_adaptor = jnp.stack(jnp.split(complete(of_adaptor), 3, axis=-1))
    grad_narrow = complete(of_narrow).T
    grad_widen = complete(of_widen).T
    return (grad_widen, grad_narrow, grad_adaptor, *head_grads)


def solution(mesh):
    placed = (
        P("dp", None),
        P(),
        P(None, "mp"),
        P("mp", None),
        P(),
        P(None, None, "mp"),
        P("mp", None),
        P("mp", None),
        P("mp", None),
        P(None, "dp", "mp"),
        P(None, "dp", "mp"),
        P(None, "dp", "mp"),
        P(),
        P(),
    )
    return jax.shard_map(
        local,
        mesh=mesh,
        in_specs=placed,
        out_specs=(
            P("mp", "dp"),
            P("mp", "dp"),
            P(None, "dp", "mp"),
            P("mp", "dp"),
            P("mp", "dp"),
            P("mp", "dp"),
        ),
        check_vma=False,
    )
```

```python
import functools

import jax
import jax.numpy as jnp
from jax import lax
from jax.experimental import pallas as pl
from jax.experimental.pallas import tpu as pltpu
from jax.sharding import PartitionSpec as P

PATCH = 32


slope_coef = 0.7978845608028654
cubic_coef = 0.044715


def smooth(value):
    return 0.5 * value * (1.0 + jnp.tanh(slope_coef * (value + cubic_coef * value * value * value)))


def smooth_slope(value):
    tangent = jnp.tanh(slope_coef * (value + cubic_coef * value * value * value))
    return 0.5 * (1.0 + tangent) + 0.5 * value * (1.0 - tangent * tangent) * slope_coef * (
        1.0 + 3.0 * cubic_coef * value * value
    )


def normalize(value, gain):
    centre = value - jnp.mean(value, axis=-1, keepdims=True)
    inverse = lax.rsqrt(jnp.mean(centre * centre, axis=-1, keepdims=True) + 1e-06)
    normal = centre * inverse
    return (normal * gain, normal, inverse)


def normalize_back(upstream, gain, normal, inverse):
    scaled = upstream * gain
    return inverse * (
        scaled
        - jnp.mean(scaled, axis=-1, keepdims=True)
        - normal * jnp.mean(scaled * normal, axis=-1, keepdims=True)
    )


def finish(product, square_student, square_target, student, target):
    joint = lax.rsqrt(square_student * square_target)
    cosine = product * joint
    slope = cosine[:, None] * student / square_student[:, None] - target * joint[:, None]
    return (cosine, slope)


def swap(value, axis, offset):
    count = lax.axis_size(axis)
    return lax.ppermute(value, axis, [(i, i ^ offset) for i in range(count)])


def ordered(value, count, position):
    cut = value.reshape((count, value.shape[0] // count) + value.shape[1:])
    return [
        lax.dynamic_index_in_dim(cut, position ^ j, 0, keepdims=False) for j in range(count)
    ]


def gather(piece, axis):
    return jnp.concatenate(
        [piece] + [swap(piece, axis, j) for j in range(1, lax.axis_size(axis))], axis=0
    )


def bits_of(count, low_first):
    bits = [1 << k for k in range(count.bit_length() - 1)]
    return bits if low_first else bits[::-1]


def scatter_begin(blocks, axis, low_first):
    bits = bits_of(len(blocks), low_first)
    leaving = [j for j in range(len(blocks)) if j & bits[0]]
    packed = jnp.concatenate([blocks[j].astype(jnp.bfloat16) for j in leaving], axis=0)
    held = {j: blocks[j] for j in range(len(blocks)) if j not in leaving}
    return [held, leaving, swap(packed, axis, bits[0])]


def scatter_rest(held, leaving, packed, axis, low_first):
    size = held[0].shape[0]
    bits = bits_of(lax.axis_size(axis), low_first)
    for bit, later in zip(bits, bits[1:]):
        for k, j in enumerate(leaving):
            piece = packed[k * size : (k + 1) * size]
            held[j ^ bit] = held[j ^ bit] + piece.astype(jnp.float32)
        leaving = [j for j in sorted(held) if j & later]
        packed = jnp.concatenate([held.pop(j).astype(jnp.bfloat16) for j in leaving], axis=0)
        packed = swap(packed, axis, later)
    return held[0], packed


def gather_doubling(piece, axis, low_first):
    held = {0: piece}
    size = piece.shape[0]
    for bit in bits_of(lax.axis_size(axis), low_first):
        order = sorted(held)
        packed = held[0] if len(order) == 1 else jnp.concatenate([held[j] for j in order], axis=0)
        packed = swap(packed, axis, bit)
        for k, j in enumerate(order):
            held[j ^ bit] = packed[k * size : (k + 1) * size]
    return jnp.concatenate([held[j] for j in sorted(held)], axis=0)


def reverse_bits(value, count):
    result = 0
    for k in range(count.bit_length() - 1):
        result = result * 2 + (value >> k) % 2
    return result


def limits(flops=0):
    return dict(
        compiler_params=pltpu.CompilerParams(vmem_limit_bytes=48 * 2**20),
        cost_estimate=pl.CostEstimate(flops=flops, bytes_accessed=0, transcendentals=0),
    )


IN_VMEM = pl.BlockSpec(memory_space=pltpu.VMEM)
IN_SMEM = pl.BlockSpec(memory_space=pltpu.SMEM)
IN_PLACE = pl.BlockSpec(memory_space=pl.ANY)


def pack_kernel(groups, images, turned, lag_ref, slot_ref, group_ref, *refs):
    count = len(turned)
    teachers, (keep_ref, send_ref) = refs[:count], refs[count : count + 2]
    held, sems = refs[count + 2 : -1], refs[-1]
    share = images // groups
    group = group_ref[0]
    copies = [
        pltpu.make_async_copy(teachers[t].at[lag_ref[t] - 1], held[t], sems.at[t])
        for t in range(count)
    ]
    for copy in copies:
        copy.start()
    slots = [slot_ref[group * images + i] for i in range(images)]
    places = []
    for i in range(images):
        rank = sum((slots[j] < slots[i]).astype(jnp.int32) for j in range(images) if j != i)
        away = lax.div(slots[i], images) ^ group
        spot = (away >> 1) * share + lax.rem(rank, share)
        places.append((away & 1, pl.ds(pl.multiple_of(spot * PATCH, PATCH), PATCH)))
    start = 0
    for t in range(count):
        copies[t].wait()
        value = held[t][...]
        if turned[t]:
            value = value.T
        columns = slice(start, start + value.shape[1])
        start += value.shape[1]
        for i, (side, to) in enumerate(places):
            piece = value[i * PATCH : (i + 1) * PATCH, :]

            @pl.when(side == 0)
            def _(piece=piece, to=to, columns=columns):
                keep_ref[to, columns] = piece

            @pl.when(side != 0)
            def _(piece=piece, to=to, columns=columns):
                send_ref[to, columns] = piece


def pack(step_lags, owner_slot, group, teachers, groups, images):
    rows = images * PATCH
    width = sum(teacher.shape[-1] for teacher in teachers)
    turned = [teacher.shape[-1] % 128 != 0 for teacher in teachers]
    teachers = [
        jnp.swapaxes(teacher, 1, 2) if turn else teacher for teacher, turn in zip(teachers, turned)
    ]
    half = jax.ShapeDtypeStruct((rows // 2, width), jnp.bfloat16)
    return pl.pallas_call(
        functools.partial(pack_kernel, groups, images, turned),
        out_shape=(half, half),
        in_specs=[IN_SMEM] * 3 + [IN_PLACE] * len(teachers),
        out_specs=(IN_VMEM, IN_VMEM),
        scratch_shapes=[pltpu.VMEM(teacher.shape[1:], jnp.bfloat16) for teacher in teachers]
        + [pltpu.SemaphoreType.DMA((len(teachers),))],
        name="pack",
        **limits(),
    )(step_lags, owner_slot, group.reshape(1), *teachers)


def place_kernel(images, place_ref, *refs):
    out_ref = refs[-1]
    each = images // (len(refs) - 1)
    for a in range(images):
        to = pl.ds(pl.multiple_of(place_ref[a] * PATCH, PATCH), PATCH)
        k = a % each
        out_ref[to, :] = refs[a // each][k * PATCH : (k + 1) * PATCH, :]


def loss_kernel(start, width, count, member_ref, *refs):
    parts, terms = refs[:count], refs[count:]
    sides = len(terms) // 3
    terms, slope_refs = terms[: 2 * sides], terms[2 * sides :]
    member = member_ref[0]
    pieces = [part[:, start : start + width].astype(jnp.float32) for part in parts]
    for bit in bits_of(count, True):
        flipped = (member & bit) != 0
        pieces = [jnp.where(flipped, pieces[j ^ bit], pieces[j]) for j in range(count)]
    target = jnp.concatenate(pieces, axis=-1)
    student = [
        terms[2 * k][...] + terms[2 * k + 1][...].astype(jnp.float32) for k in range(sides)
    ]
    student = student[0] if sides == 1 else jnp.concatenate(student, axis=-1)
    product = jnp.sum(student * target, axis=-1, keepdims=True)
    square_student = jnp.sum(student * student, axis=-1, keepdims=True) + 1e-06
    square_target = jnp.sum(target * target, axis=-1, keepdims=True) + 1e-06
    joint = lax.rsqrt(square_student * square_target)
    cosine = product * joint
    slope = ((cosine / square_student) * student - target * joint).astype(jnp.bfloat16)
    wide = slope.shape[1] // sides
    for k in range(sides):
        slope_refs[k][...] = slope[:, k * wide : (k + 1) * wide]


def loss(member, terms, parts, start, width):
    flat = [value for pair in terms for value in pair]
    return pl.pallas_call(
        functools.partial(loss_kernel, start, width, len(parts)),
        out_shape=[jax.ShapeDtypeStruct(last.shape, jnp.bfloat16) for _, last in terms],
        in_specs=[IN_SMEM] + [IN_VMEM] * (len(parts) + len(flat)),
        out_specs=[IN_VMEM] * len(terms),
        name="loss",
        **limits(),
    )(member.reshape(1), *parts, *flat)


def beside(refs):
    return refs[0][...] if len(refs) == 1 else jnp.concatenate([r[...] for r in refs], axis=1)


def product_kernel(groups, shape, spot_ref, *refs):
    keep_ref, send_ref = refs[-2:]
    side, base = spot_ref[0] != 0, spot_ref[1]
    tall = keep_ref.shape[1]
    used = column = 0
    for lefts, rights in shape:
        left = beside(refs[used : used + lefts])
        right = beside(refs[used + lefts : used + lefts + rights])
        used += lefts + rights
        cut, wide = left.shape[1] // groups, right.shape[1]
        columns = slice(column, column + wide)
        column += wide
        full = lax.dot_general(
            left, right, (((0,), (0,)), ((), ())), preferred_element_type=jnp.float32
        )
        for pair in range(groups // 2):
            even = full[2 * pair * cut : (2 * pair + 1) * cut, :]
            odd = full[(2 * pair + 1) * cut : (2 * pair + 2) * cut, :]
            at = base ^ reverse_bits(pair, groups // 2)
            if cut < tall:
                rest = jnp.zeros((tall - cut, wide), jnp.float32)
                even = jnp.concatenate([even, rest], axis=0)
                odd = jnp.concatenate([odd, rest], axis=0)
            keep_ref[at, :, columns] = jnp.where(side, odd, even).astype(jnp.bfloat16)
            send_ref[at, :, columns] = jnp.where(side, even, odd).astype(jnp.bfloat16)


def product(pairs, groups, group):
    talls = [sum(left.shape[1] for left in lefts) for lefts, _ in pairs]
    wides = [sum(right.shape[1] for right in rights) for _, rights in pairs]
    tall, wide = max(talls) // groups, sum(wides)
    half = jax.ShapeDtypeStruct((groups // 2, tall, wide), jnp.bfloat16)
    spot = jnp.stack([group % 2, reverse_bits(group // 2, groups // 2)]).astype(jnp.int32)
    flat = [value for lefts, rights in pairs for value in (*lefts, *rights)]
    return pl.pallas_call(
        functools.partial(product_kernel, groups, [(len(l), len(r)) for l, r in pairs]),
        out_shape=(half, half),
        in_specs=[IN_SMEM] + [IN_VMEM] * len(flat),
        out_specs=(IN_VMEM, IN_VMEM),
        name="product",
        **limits(),
    )(spot, *flat)


def pin(*values):
    return lax.optimization_barrier(values)


def merge_kernel(held_ref, came_ref, kept_ref, sent_ref):
    half = kept_ref.shape[0]
    for k in range(half):
        low = held_ref[k].astype(jnp.float32) + came_ref[k].astype(jnp.float32)
        high = held_ref[half + k].astype(jnp.float32) + came_ref[half + k].astype(jnp.float32)
        kept_ref[k] = low
        sent_ref[k] = high.astype(jnp.bfloat16)


def merge(held, came):
    shape = (held.shape[0] // 2, *held.shape[1:])
    return pl.pallas_call(
        merge_kernel,
        out_shape=(
            jax.ShapeDtypeStruct(shape, jnp.float32),
            jax.ShapeDtypeStruct(shape, jnp.bfloat16),
        ),
        in_specs=[IN_VMEM, IN_VMEM],
        out_specs=(IN_VMEM, IN_VMEM),
        name="merge",
        **limits(2**35),
    )(held, came)


def begin(halves):
    keep, send = halves
    bits = bits_of(2 * keep.shape[0], True)[1:]
    return (keep, swap(send, "dp", 1), bits)


def advance(state, kernel=False):
    keep, came, bits = state
    if not bits:
        return state
    if kernel:
        kept, sent = merge(keep, came)
    else:
        held = keep.astype(jnp.float32) + came.astype(jnp.float32)
        half = held.shape[0] // 2
        kept, sent = held[:half], held[half:].astype(jnp.bfloat16)
    return (kept, swap(sent, "dp", bits[0]), bits[1:])


def finish_kernel(cuts, *refs):
    count = len(cuts)
    outs = refs[2 * count :]
    used = 0
    for k in range(count):
        total = refs[2 * k][0].astype(jnp.float32) + refs[2 * k + 1][0].astype(jnp.float32)
        for rows, start, end in cuts[k]:
            outs[used][...] = total[:rows, start:end]
            used += 1


def finish(states, cuts):
    for state in states:
        assert not state[2]
    return pl.pallas_call(
        functools.partial(finish_kernel, cuts),
        out_shape=[
            jax.ShapeDtypeStruct((rows, end - start), jnp.float32)
            for cut in cuts
            for rows, start, end in cut
        ],
        in_specs=[IN_VMEM] * (2 * len(states)),
        out_specs=[IN_VMEM] * sum(len(cut) for cut in cuts),
        name="finish",
        **limits(2**35),
    )(*[value for state in states for value in state[:2]])


def settle(state, kernel=False):
    while state[2]:
        state = advance(state, kernel)
    return state


def arrive(state, came):
    return (state[0], came, state[2])


def local(
    tokens,
    norm_gain,
    widen_weight,
    narrow_weight,
    final_gain,
    adaptor_in,
    head_dino,
    head_siglip,
    head_sam,
    teacher_dino,
    teacher_siglip,
    teacher_sam,
    step_lags,
    owner_slot,
):
    groups = lax.axis_size("dp")
    members = lax.axis_size("mp")
    group = lax.axis_index("dp")
    member = lax.axis_index("mp")
    rows = tokens.shape[0]
    images = rows // PATCH
    share = images // groups
    block = rows // members
    heads = (head_dino, head_siglip, head_sam)
    teachers = (teacher_dino, teacher_siglip, teacher_sam)
    widths = [teacher.shape[-1] for teacher in teachers]
    exact = dict(preferred_element_type=jnp.float32)

    slots = owner_slot.reshape(groups, images)
    rank = jnp.sum(slots[:, :, None] > slots[:, None, :], axis=2, dtype=jnp.int32) % share
    source = lax.broadcasted_iota(jnp.int32, (groups, images), 0)
    landing = (source ^ group) * share + rank
    slot_rows = group * images + lax.broadcasted_iota(jnp.int32, (images,), 0)
    found = slots.reshape(1, -1) == slot_rows[:, None]
    landed = jnp.sum(jnp.where(found, landing.reshape(1, -1), 0), axis=1)
    position = lax.broadcasted_iota(jnp.int32, (images,), 0) ^ (member * (images // members))
    at = lax.broadcasted_iota(jnp.int32, (images, images), 0)
    place = jnp.sum(jnp.where(landed[None, :] == at, position[None, :], 0), axis=1)

    tokens = jnp.concatenate(ordered(tokens, members, member), axis=0)
    first, _, _ = normalize(tokens.astype(jnp.float32), norm_gain)
    first = lax.optimization_barrier(first.astype(jnp.bfloat16))
    widened = jnp.dot(first, widen_weight, **exact)
    active = smooth(widened).astype(jnp.bfloat16)
    mixed = jnp.dot(active, narrow_weight, **exact).reshape(members, block, -1)
    mixed, step_lags = pin(mixed, step_lags)
    came = [swap(mixed[j].astype(jnp.bfloat16), "mp", j) for j in range(1, members)]
    kept, crossing = pack(step_lags, owner_slot, group, teachers, groups, images)
    came[0], crossing = pin(came[0], swap(crossing, "dp", 1))
    hidden = tokens[:block].astype(jnp.float32) + mixed[0]
    for piece in came:
        hidden = hidden + piece.astype(jnp.float32)
    pairs = jnp.stack(
        [
            kept.reshape(groups // 2, share * PATCH, -1),
            crossing.reshape(groups // 2, share * PATCH, -1),
        ],
        axis=1,
    ).reshape(groups // 2, 2 * share * PATCH, -1)
    arrived = [pairs[0]] + [swap(pairs[o], "dp", 2 * o) for o in range(1, groups // 2)]
    owned = pl.pallas_call(
        functools.partial(place_kernel, images),
        out_shape=jax.ShapeDtypeStruct((rows, sum(widths)), jnp.bfloat16),
        in_specs=[IN_SMEM] + [IN_VMEM] * len(arrived),
        out_specs=IN_VMEM,
        name="place",
        **limits(),
    )(place, *arrived)

    final_rows, normal_rows, inverse_rows = normalize(hidden, final_gain)
    final = gather(final_rows.astype(jnp.bfloat16), "mp")

    owned = owned.reshape(members, block, -1)
    parts = [owned[0]] + [swap(owned[j], "mp", j) for j in range(1, members)]

    ways = ((True, False), (True,), (False,))
    befores, lifteds, students = [], [], []
    for index in range(3):
        before = jnp.dot(final, adaptor_in[index], **exact)
        lifted = smooth(before).astype(jnp.bfloat16)
        partial = jnp.dot(lifted, heads[index], **exact).reshape(members, block, -1)
        if index < 2:
            final, partial = pin(final, partial)
        befores.append(before)
        lifteds.append(lifted)
        wide = partial.shape[-1] // len(ways[index])
        students.append(
            [
                scatter_begin(list(partial[:, :, k * wide : (k + 1) * wide]), "mp", way)
                for k, way in enumerate(ways[index])
            ]
        )
    students[0][0][2], parts[0] = pin(students[0][0][2], parts[0])
    students = [
        [scatter_rest(*term, "mp", way) for term, way in zip(terms, ways[index])]
        for index, terms in enumerate(students)
    ]
    slopes = []
    start = 0
    for index in range(3):
        made = loss(member, students[index], parts, start, widths[index])
        start += widths[index]
        slopes.append([gather_doubling(s, "mp", way) for s, way in zip(made, ways[index])])
    inners = []
    upstream = 0.0
    for index in range(3):
        back = 0.0
        wide = slopes[index][0].shape[1]
        for k, slope in enumerate(slopes[index]):
            head = heads[index][:, k * wide : (k + 1) * wide]
            back = back + jnp.einsum("rc,hc->rh", slope, head, **exact)
        inner = (back * smooth_slope(befores[index])).astype(jnp.bfloat16)
        inners.append(inner)
        upstream = upstream + jnp.einsum("rh,dh->rd", inner, adaptor_in[index], **exact)
        if index == 1:
            pairs = [(slopes[k], lifteds[k : k + 1]) for k in range(2)]
            of_heads = begin(product(pairs, groups, group))
            slopes[2][0], arrived = pin(slopes[2][0], of_heads[1])
            of_heads = advance(arrive(of_heads, arrived))
    upstream = upstream.reshape(members, block, -1)
    came = [swap(upstream[j].astype(jnp.bfloat16), "mp", j) for j in range(1, members)]

    mine, *inners = pin(upstream[0], *inners)
    of_rest = begin(
        product([([final], inners), (slopes[2], lifteds[2:])], groups, group)
    )
    came[0], one, two = pin(came[0], of_heads[1], of_rest[1])
    of_heads = advance(arrive(of_heads, one))
    of_rest = advance(arrive(of_rest, two))
    total = mine
    for piece in came:
        total = total + piece.astype(jnp.float32)
    through_rows = normalize_back(total, final_gain, normal_rows, inverse_rows)
    through_rows = through_rows.astype(jnp.bfloat16)
    came = [swap(through_rows, "mp", j) for j in range(1, members)]
    came[-1], one = pin(came[-1], of_rest[1])
    of_rest = advance(arrive(of_rest, one))
    through = jnp.concatenate([through_rows, *came], axis=0)

    of_narrow = begin(product([([through], [active])], groups, group))
    back_two = jnp.einsum("rd,fd->rf", through, narrow_weight, **exact)
    inner_two = (back_two * smooth_slope(widened)).astype(jnp.bfloat16)
    inner_two, one = pin(inner_two, of_narrow[1])
    of_narrow = advance(arrive(of_narrow, one), True)
    of_widen = advance(begin(product([([first], [inner_two])], groups, group)), True)
    of_narrow = settle(of_narrow, True)
    of_widen = settle(of_widen, True)
    of_heads, of_rest = settle(of_heads), settle(of_rest)
    keep, *landed = pin(of_widen[0], of_narrow[1], of_heads[1], of_rest[1])
    of_widen = (keep, *of_widen[1:])
    of_narrow, of_heads, of_rest = [
        arrive(state, one) for state, one in zip((of_narrow, of_heads, of_rest), landed)
    ]
    wide = lifteds[0].shape[1]
    cuts = [head.shape[1] // groups for head in heads]
    deep = final.shape[1] // groups
    spans = [(k * wide, (k + 1) * wide) for k in range(4)]
    made = finish(
        [of_heads, of_rest, of_narrow],
        [
            [(cuts[0], *spans[0]), (cuts[1], *spans[1])],
            [(deep, *span) for span in spans[:3]] + [(cuts[2], *spans[3])],
            [(deep, 0, active.shape[1])],
        ],
    )
    head_grads = [made[0].T, made[1].T, made[5].T]
    grad_adaptor = jnp.stack(made[2:5])
    grad_narrow = made[6].T
    keep, came, _ = of_widen
    grad_widen = (keep[0].astype(jnp.float32) + came[0].astype(jnp.float32)).T
    return (grad_widen, grad_narrow, grad_adaptor, *head_grads)


def solution(mesh):
    placed = (
        P("dp", None),
        P(),
        P(None, "mp"),
        P("mp", None),
        P(),
        P(None, None, "mp"),
        P("mp", None),
        P("mp", None),
        P("mp", None),
        P(None, "dp", "mp"),
        P(None, "dp", "mp"),
        P(None, "dp", "mp"),
        P(),
        P(),
    )
    return jax.shard_map(
        local,
        mesh=mesh,
        in_specs=placed,
        out_specs=(
            P("mp", "dp"),
            P("mp", "dp"),
            P(None, "dp", "mp"),
            P("mp", "dp"),
            P("mp", "dp"),
            P("mp", "dp"),
        ),
        check_vma=False,
    )
```

```python
import functools

import jax
import jax.numpy as jnp
from jax import lax
from jax.experimental import pallas as pl
from jax.experimental.pallas import tpu as pltpu
from jax.sharding import PartitionSpec as P

PATCH = 32


slope_coef = 0.7978845608028654
cubic_coef = 0.044715


def smooth(value):
    return 0.5 * value * (1.0 + jnp.tanh(slope_coef * (value + cubic_coef * value * value * value)))


def smooth_slope(value):
    tangent = jnp.tanh(slope_coef * (value + cubic_coef * value * value * value))
    return 0.5 * (1.0 + tangent) + 0.5 * value * (1.0 - tangent * tangent) * slope_coef * (
        1.0 + 3.0 * cubic_coef * value * value
    )


def normalize(value, gain):
    centre = value - jnp.mean(value, axis=-1, keepdims=True)
    inverse = lax.rsqrt(jnp.mean(centre * centre, axis=-1, keepdims=True) + 1e-06)
    normal = centre * inverse
    return (normal * gain, normal, inverse)


def normalize_back(upstream, gain, normal, inverse):
    scaled = upstream * gain
    return inverse * (
        scaled
        - jnp.mean(scaled, axis=-1, keepdims=True)
        - normal * jnp.mean(scaled * normal, axis=-1, keepdims=True)
    )


def finish(product, square_student, square_target, student, target):
    joint = lax.rsqrt(square_student * square_target)
    cosine = product * joint
    slope = cosine[:, None] * student / square_student[:, None] - target * joint[:, None]
    return (cosine, slope)


def swap(value, axis, offset):
    count = lax.axis_size(axis)
    return lax.ppermute(value, axis, [(i, i ^ offset) for i in range(count)])


def ordered(value, count, position):
    cut = value.reshape((count, value.shape[0] // count) + value.shape[1:])
    return [
        lax.dynamic_index_in_dim(cut, position ^ j, 0, keepdims=False) for j in range(count)
    ]


def gather(piece, axis):
    return jnp.concatenate(
        [piece] + [swap(piece, axis, j) for j in range(1, lax.axis_size(axis))], axis=0
    )


def bits_of(count, low_first):
    bits = [1 << k for k in range(count.bit_length() - 1)]
    return bits if low_first else bits[::-1]


def scatter_begin(blocks, axis, low_first):
    bits = bits_of(len(blocks), low_first)
    leaving = [j for j in range(len(blocks)) if j & bits[0]]
    packed = jnp.concatenate([blocks[j].astype(jnp.bfloat16) for j in leaving], axis=0)
    held = {j: blocks[j] for j in range(len(blocks)) if j not in leaving}
    return [held, leaving, swap(packed, axis, bits[0])]


def scatter_rest(held, leaving, packed, axis, low_first):
    size = held[0].shape[0]
    bits = bits_of(lax.axis_size(axis), low_first)
    for bit, later in zip(bits, bits[1:]):
        for k, j in enumerate(leaving):
            piece = packed[k * size : (k + 1) * size]
            held[j ^ bit] = held[j ^ bit] + piece.astype(jnp.float32)
        leaving = [j for j in sorted(held) if j & later]
        packed = jnp.concatenate([held.pop(j).astype(jnp.bfloat16) for j in leaving], axis=0)
        packed = swap(packed, axis, later)
    return held[0], packed


def gather_doubling(piece, axis, low_first):
    held = {0: piece}
    size = piece.shape[0]
    for bit in bits_of(lax.axis_size(axis), low_first):
        order = sorted(held)
        packed = held[0] if len(order) == 1 else jnp.concatenate([held[j] for j in order], axis=0)
        packed = swap(packed, axis, bit)
        for k, j in enumerate(order):
            held[j ^ bit] = packed[k * size : (k + 1) * size]
    return jnp.concatenate([held[j] for j in sorted(held)], axis=0)


def reverse_bits(value, count):
    result = 0
    for k in range(count.bit_length() - 1):
        result = result * 2 + (value >> k) % 2
    return result


def limits(flops=0):
    return dict(
        compiler_params=pltpu.CompilerParams(vmem_limit_bytes=48 * 2**20),
        cost_estimate=pl.CostEstimate(flops=flops, bytes_accessed=0, transcendentals=0),
    )


IN_VMEM = pl.BlockSpec(memory_space=pltpu.VMEM)
IN_SMEM = pl.BlockSpec(memory_space=pltpu.SMEM)
IN_PLACE = pl.BlockSpec(memory_space=pl.ANY)


def pack_kernel(groups, images, turned, lag_ref, slot_ref, group_ref, *refs):
    count = len(turned)
    teachers, (keep_ref, send_ref) = refs[:count], refs[count : count + 2]
    held, sems = refs[count + 2 : -1], refs[-1]
    share = images // groups
    group = group_ref[0]
    copies = [
        pltpu.make_async_copy(teachers[t].at[lag_ref[t] - 1], held[t], sems.at[t])
        for t in range(count)
    ]
    for copy in copies:
        copy.start()
    slots = [slot_ref[group * images + i] for i in range(images)]
    places = []
    for i in range(images):
        rank = sum((slots[j] < slots[i]).astype(jnp.int32) for j in range(images) if j != i)
        away = lax.div(slots[i], images) ^ group
        spot = (away >> 1) * share + lax.rem(rank, share)
        places.append((away & 1, pl.ds(pl.multiple_of(spot * PATCH, PATCH), PATCH)))
    start = 0
    for t in range(count):
        copies[t].wait()
        value = held[t][...]
        if turned[t]:
            value = value.T
        columns = slice(start, start + value.shape[1])
        start += value.shape[1]
        for i, (side, to) in enumerate(places):
            piece = value[i * PATCH : (i + 1) * PATCH, :]

            @pl.when(side == 0)
            def _(piece=piece, to=to, columns=columns):
                keep_ref[to, columns] = piece

            @pl.when(side != 0)
            def _(piece=piece, to=to, columns=columns):
                send_ref[to, columns] = piece


def pack(step_lags, owner_slot, group, teachers, groups, images):
    rows = images * PATCH
    width = sum(teacher.shape[-1] for teacher in teachers)
    turned = [teacher.shape[-1] % 128 != 0 for teacher in teachers]
    teachers = [
        jnp.swapaxes(teacher, 1, 2) if turn else teacher for teacher, turn in zip(teachers, turned)
    ]
    half = jax.ShapeDtypeStruct((rows // 2, width), jnp.bfloat16)
    return pl.pallas_call(
        functools.partial(pack_kernel, groups, images, turned),
        out_shape=(half, half),
        in_specs=[IN_SMEM] * 3 + [IN_PLACE] * len(teachers),
        out_specs=(IN_VMEM, IN_VMEM),
        scratch_shapes=[pltpu.VMEM(teacher.shape[1:], jnp.bfloat16) for teacher in teachers]
        + [pltpu.SemaphoreType.DMA((len(teachers),))],
        name="pack",
        **limits(),
    )(step_lags, owner_slot, group.reshape(1), *teachers)


def place_kernel(images, place_ref, *refs):
    out_ref = refs[-1]
    each = images // (len(refs) - 1)
    for a in range(images):
        to = pl.ds(pl.multiple_of(place_ref[a] * PATCH, PATCH), PATCH)
        k = a % each
        out_ref[to, :] = refs[a // each][k * PATCH : (k + 1) * PATCH, :]


def loss_kernel(start, width, count, member_ref, *refs):
    parts, terms = refs[:count], refs[count:]
    sides = len(terms) // 3
    terms, slope_refs = terms[: 2 * sides], terms[2 * sides :]
    member = member_ref[0]
    pieces = [part[:, start : start + width].astype(jnp.float32) for part in parts]
    for bit in bits_of(count, True):
        flipped = (member & bit) != 0
        pieces = [jnp.where(flipped, pieces[j ^ bit], pieces[j]) for j in range(count)]
    target = jnp.concatenate(pieces, axis=-1)
    student = [
        terms[2 * k][...] + terms[2 * k + 1][...].astype(jnp.float32) for k in range(sides)
    ]
    student = student[0] if sides == 1 else jnp.concatenate(student, axis=-1)
    product = jnp.sum(student * target, axis=-1, keepdims=True)
    square_student = jnp.sum(student * student, axis=-1, keepdims=True) + 1e-06
    square_target = jnp.sum(target * target, axis=-1, keepdims=True) + 1e-06
    joint = lax.rsqrt(square_student * square_target)
    cosine = product * joint
    slope = ((cosine / square_student) * student - target * joint).astype(jnp.bfloat16)
    wide = slope.shape[1] // sides
    for k in range(sides):
        slope_refs[k][...] = slope[:, k * wide : (k + 1) * wide]


def loss(member, terms, parts, start, width):
    flat = [value for pair in terms for value in pair]
    return pl.pallas_call(
        functools.partial(loss_kernel, start, width, len(parts)),
        out_shape=[jax.ShapeDtypeStruct(last.shape, jnp.bfloat16) for _, last in terms],
        in_specs=[IN_SMEM] + [IN_VMEM] * (len(parts) + len(flat)),
        out_specs=[IN_VMEM] * len(terms),
        name="loss",
        **limits(),
    )(member.reshape(1), *parts, *flat)


def beside(refs):
    return refs[0][...] if len(refs) == 1 else jnp.concatenate([r[...] for r in refs], axis=1)


def product_kernel(groups, shape, spot_ref, *refs):
    keep_ref, send_ref = refs[-2:]
    side, base = spot_ref[0] != 0, spot_ref[1]
    tall = keep_ref.shape[1]
    used = column = 0
    for lefts, rights in shape:
        left = beside(refs[used : used + lefts])
        right = beside(refs[used + lefts : used + lefts + rights])
        used += lefts + rights
        cut, wide = left.shape[1] // groups, right.shape[1]
        columns = slice(column, column + wide)
        column += wide
        full = lax.dot_general(
            left, right, (((0,), (0,)), ((), ())), preferred_element_type=jnp.float32
        )
        for pair in range(groups // 2):
            even = full[2 * pair * cut : (2 * pair + 1) * cut, :]
            odd = full[(2 * pair + 1) * cut : (2 * pair + 2) * cut, :]
            at = base ^ reverse_bits(pair, groups // 2)
            if cut < tall:
                rest = jnp.zeros((tall - cut, wide), jnp.float32)
                even = jnp.concatenate([even, rest], axis=0)
                odd = jnp.concatenate([odd, rest], axis=0)
            keep_ref[at, :, columns] = jnp.where(side, odd, even).astype(jnp.bfloat16)
            send_ref[at, :, columns] = jnp.where(side, even, odd).astype(jnp.bfloat16)


def product(pairs, groups, group, flops=0):
    talls = [sum(left.shape[1] for left in lefts) for lefts, _ in pairs]
    wides = [sum(right.shape[1] for right in rights) for _, rights in pairs]
    tall, wide = max(talls) // groups, sum(wides)
    half = jax.ShapeDtypeStruct((groups // 2, tall, wide), jnp.bfloat16)
    spot = jnp.stack([group % 2, reverse_bits(group // 2, groups // 2)]).astype(jnp.int32)
    flat = [value for lefts, rights in pairs for value in (*lefts, *rights)]
    return pl.pallas_call(
        functools.partial(product_kernel, groups, [(len(l), len(r)) for l, r in pairs]),
        out_shape=(half, half),
        in_specs=[IN_SMEM] + [IN_VMEM] * len(flat),
        out_specs=(IN_VMEM, IN_VMEM),
        name="product",
        **limits(flops),
    )(spot, *flat)


def narrow_kernel(count, group_ref, active_ref, *refs):
    out_ref = refs[-1]
    columns = jnp.concatenate([ref[0] for ref in refs[:count]], axis=1)
    term = jnp.dot(columns, active_ref[0], preferred_element_type=jnp.float32)

    @pl.when(pl.program_id(0) == 0)
    def _():
        out_ref[...] = term

    @pl.when(pl.program_id(0) != 0)
    def _():
        out_ref[...] += term


def narrow_sum(group, actives, columns):
    groups, rows, units = actives.shape
    cut = columns[0].shape[1]
    return pl.pallas_call(
        functools.partial(narrow_kernel, len(columns)),
        out_shape=jax.ShapeDtypeStruct((cut, units), jnp.float32),
        grid_spec=pltpu.PrefetchScalarGridSpec(
            num_scalar_prefetch=1,
            grid=(groups,),
            in_specs=[pl.BlockSpec((1, rows, units), lambda o, g: (o ^ g[0], 0, 0))]
            + [pl.BlockSpec((1, cut, column.shape[2]), lambda o, g: (o, 0, 0)) for column in columns],
            out_specs=pl.BlockSpec((cut, units), lambda o, g: (0, 0)),
        ),
        name="narrow",
        **limits(2**35),
    )(group.reshape(1), actives, *columns)


def pin(*values):
    return lax.optimization_barrier(values)


def merge_kernel(held_ref, came_ref, kept_ref, sent_ref):
    half = kept_ref.shape[0]
    for k in range(half):
        low = held_ref[k].astype(jnp.float32) + came_ref[k].astype(jnp.float32)
        high = held_ref[half + k].astype(jnp.float32) + came_ref[half + k].astype(jnp.float32)
        kept_ref[k] = low
        sent_ref[k] = high.astype(jnp.bfloat16)


def merge(held, came):
    shape = (held.shape[0] // 2, *held.shape[1:])
    return pl.pallas_call(
        merge_kernel,
        out_shape=(
            jax.ShapeDtypeStruct(shape, jnp.float32),
            jax.ShapeDtypeStruct(shape, jnp.bfloat16),
        ),
        in_specs=[IN_VMEM, IN_VMEM],
        out_specs=(IN_VMEM, IN_VMEM),
        name="merge",
        **limits(2**35),
    )(held, came)


def begin(halves):
    keep, send = halves
    bits = bits_of(2 * keep.shape[0], True)[1:]
    return (keep, swap(send, "dp", 1), bits)


def advance(state, kernel=False):
    keep, came, bits = state
    if not bits:
        return state
    if kernel:
        kept, sent = merge(keep, came)
    else:
        held = keep.astype(jnp.float32) + came.astype(jnp.float32)
        half = held.shape[0] // 2
        kept, sent = held[:half], held[half:].astype(jnp.bfloat16)
    return (kept, swap(sent, "dp", bits[0]), bits[1:])


def finish_kernel(cuts, *refs):
    count = len(cuts)
    outs = refs[2 * count :]
    used = 0
    for k in range(count):
        total = refs[2 * k][0].astype(jnp.float32) + refs[2 * k + 1][0].astype(jnp.float32)
        for rows, start, end in cuts[k]:
            outs[used][...] = total[:rows, start:end]
            used += 1


def finish(states, cuts):
    for state in states:
        assert not state[2]
    return pl.pallas_call(
        functools.partial(finish_kernel, cuts),
        out_shape=[
            jax.ShapeDtypeStruct((rows, end - start), jnp.float32)
            for cut in cuts
            for rows, start, end in cut
        ],
        in_specs=[IN_VMEM] * (2 * len(states)),
        out_specs=[IN_VMEM] * sum(len(cut) for cut in cuts),
        name="finish",
        **limits(2**35),
    )(*[value for state in states for value in state[:2]])


def settle(state, kernel=False):
    while state[2]:
        state = advance(state, kernel)
    return state


def arrive(state, came):
    return (state[0], came, state[2])


def local(
    tokens,
    norm_gain,
    widen_weight,
    narrow_weight,
    final_gain,
    adaptor_in,
    head_dino,
    head_siglip,
    head_sam,
    teacher_dino,
    teacher_siglip,
    teacher_sam,
    step_lags,
    owner_slot,
):
    groups = lax.axis_size("dp")
    members = lax.axis_size("mp")
    group = lax.axis_index("dp")
    member = lax.axis_index("mp")
    rows = tokens.shape[0]
    images = rows // PATCH
    share = images // groups
    block = rows // members
    heads = (head_dino, head_siglip, head_sam)
    teachers = (teacher_dino, teacher_siglip, teacher_sam)
    widths = [teacher.shape[-1] for teacher in teachers]
    exact = dict(preferred_element_type=jnp.float32)

    slots = owner_slot.reshape(groups, images)
    rank = jnp.sum(slots[:, :, None] > slots[:, None, :], axis=2, dtype=jnp.int32) % share
    source = lax.broadcasted_iota(jnp.int32, (groups, images), 0)
    landing = (source ^ group) * share + rank
    slot_rows = group * images + lax.broadcasted_iota(jnp.int32, (images,), 0)
    found = slots.reshape(1, -1) == slot_rows[:, None]
    landed = jnp.sum(jnp.where(found, landing.reshape(1, -1), 0), axis=1)
    position = lax.broadcasted_iota(jnp.int32, (images,), 0) ^ (member * (images // members))
    at = lax.broadcasted_iota(jnp.int32, (images, images), 0)
    place = jnp.sum(jnp.where(landed[None, :] == at, position[None, :], 0), axis=1)

    tokens = jnp.concatenate(ordered(tokens, members, member), axis=0)
    first, _, _ = normalize(tokens.astype(jnp.float32), norm_gain)
    first = lax.optimization_barrier(first.astype(jnp.bfloat16))
    widened = jnp.dot(first, widen_weight, **exact)
    active = smooth(widened).astype(jnp.bfloat16)
    mixed = jnp.dot(active, narrow_weight, **exact).reshape(members, block, -1)
    mixed, step_lags = pin(mixed, step_lags)
    came = [swap(mixed[j].astype(jnp.bfloat16), "mp", j) for j in range(1, members)]
    kept, crossing = pack(step_lags, owner_slot, group, teachers, groups, images)
    came[0], crossing = pin(came[0], swap(crossing, "dp", 1))
    hidden = tokens[:block].astype(jnp.float32) + mixed[0]
    for piece in came:
        hidden = hidden + piece.astype(jnp.float32)
    pairs = jnp.stack(
        [
            kept.reshape(groups // 2, share * PATCH, -1),
            crossing.reshape(groups // 2, share * PATCH, -1),
        ],
        axis=1,
    ).reshape(groups // 2, 2 * share * PATCH, -1)
    arrived = [pairs[0]] + [swap(pairs[o], "dp", 2 * o) for o in range(1, groups // 2)]
    owned = pl.pallas_call(
        functools.partial(place_kernel, images),
        out_shape=jax.ShapeDtypeStruct((rows, sum(widths)), jnp.bfloat16),
        in_specs=[IN_SMEM] + [IN_VMEM] * len(arrived),
        out_specs=IN_VMEM,
        name="place",
        **limits(),
    )(place, *arrived)

    final_rows, normal_rows, inverse_rows = normalize(hidden, final_gain)
    final = gather(final_rows.astype(jnp.bfloat16), "mp")
    final, late, own = pin(final, active, owned[:block])
    actives = lax.all_gather(late, "dp")

    owned = owned.reshape(members, block, -1)
    parts = [own] + [swap(owned[j], "mp", j) for j in range(1, members)]

    ways = ((True, False), (True,), (False,))
    befores, lifteds, students = [], [], []
    for index in range(3):
        before = jnp.dot(final, adaptor_in[index], **exact)
        lifted = smooth(before).astype(jnp.bfloat16)
        partial = jnp.dot(lifted, heads[index], **exact).reshape(members, block, -1)
        if index < 2:
            final, partial = pin(final, partial)
        befores.append(before)
        lifteds.append(lifted)
        wide = partial.shape[-1] // len(ways[index])
        students.append(
            [
                scatter_begin(list(partial[:, :, k * wide : (k + 1) * wide]), "mp", way)
                for k, way in enumerate(ways[index])
            ]
        )
    students[0][0][2], parts[0] = pin(students[0][0][2], parts[0])
    students = [
        [scatter_rest(*term, "mp", way) for term, way in zip(terms, ways[index])]
        for index, terms in enumerate(students)
    ]
    slopes = []
    start = 0
    for index in range(3):
        made = loss(member, students[index], parts, start, widths[index])
        start += widths[index]
        slopes.append([gather_doubling(s, "mp", way) for s, way in zip(made, ways[index])])
    inners = []
    upstream = 0.0
    for index in range(3):
        back = 0.0
        wide = slopes[index][0].shape[1]
        for k, slope in enumerate(slopes[index]):
            head = heads[index][:, k * wide : (k + 1) * wide]
            back = back + jnp.einsum("rc,hc->rh", slope, head, **exact)
        inner = (back * smooth_slope(befores[index])).astype(jnp.bfloat16)
        inners.append(inner)
        upstream = upstream + jnp.einsum("rh,dh->rd", inner, adaptor_in[index], **exact)
        if index == 1:
            pairs = [(slopes[k], lifteds[k : k + 1]) for k in range(2)]
            of_heads = begin(product(pairs, groups, group))
            slopes[2][0], arrived = pin(slopes[2][0], of_heads[1])
            of_heads = advance(arrive(of_heads, arrived))
    upstream = upstream.reshape(members, block, -1)
    came = [swap(upstream[j].astype(jnp.bfloat16), "mp", j) for j in range(1, members)]

    mine, *inners = pin(upstream[0], *inners)
    of_rest = begin(
        product([([final], inners), (slopes[2], lifteds[2:])], groups, group)
    )
    came[0], one, two = pin(came[0], of_heads[1], of_rest[1])
    of_heads = advance(arrive(of_heads, one))
    of_rest = advance(arrive(of_rest, two))
    total = mine
    for piece in came:
        total = total + piece.astype(jnp.float32)
    through_rows = normalize_back(total, final_gain, normal_rows, inverse_rows)
    through_rows = through_rows.astype(jnp.bfloat16)
    came = [swap(through_rows, "mp", j) for j in range(1, members)]
    turned = through_rows.T.reshape(groups, -1, block)
    turned = [lax.dynamic_index_in_dim(turned, group ^ o, 0) for o in range(groups)]
    odd = swap(jnp.concatenate(turned[1::2], axis=0), "dp", 1)
    came[-1], odd, one, actives = pin(came[-1], odd, of_rest[1], actives)
    of_rest = advance(arrive(of_rest, one))
    through = jnp.concatenate([through_rows, *came], axis=0)
    both = [jnp.concatenate([turned[2 * o], odd[o : o + 1]]) for o in range(groups // 2)]
    both = [both[0]] + [swap(both[o], "dp", 2 * o) for o in range(1, groups // 2)]

    back_two = jnp.einsum("rd,fd->rf", through, narrow_weight, **exact)
    inner_two = (back_two * smooth_slope(widened)).astype(jnp.bfloat16)
    of_heads = settle(of_heads)
    inner_two, one, two = pin(inner_two, of_heads[1], of_rest[0])
    of_heads, of_rest = arrive(of_heads, one), (two, *of_rest[1:])
    of_widen = begin(product([([first], [inner_two])], groups, group, 2**35))
    of_widen = advance(of_widen, True)
    keep, *both = pin(of_widen[0], *both)
    of_widen = (keep, *of_widen[1:])
    columns = jnp.concatenate(both, axis=0)
    columns = [columns] + [swap(columns, "mp", j) for j in range(1, members)]
    of_heads, of_rest = settle(of_heads), settle(of_rest)
    while of_widen[2]:
        one, two, *columns[1:] = pin(of_widen[1], of_rest[1], *columns[1:])
        of_widen, of_rest = arrive(of_widen, one), arrive(of_rest, two)
        of_widen = advance(of_widen, True)
    wide = lifteds[0].shape[1]
    cuts = [head.shape[1] // groups for head in heads]
    deep = final.shape[1] // groups
    spans = [(k * wide, (k + 1) * wide) for k in range(4)]
    made = finish(
        [of_heads, of_rest],
        [
            [(cuts[0], *spans[0]), (cuts[1], *spans[1])],
            [(deep, *span) for span in spans[:3]] + [(cuts[2], *spans[3])],
        ],
    )
    head_grads = [made[0].T, made[1].T, made[5].T]
    grad_adaptor = jnp.stack(made[2:5])
    grad_narrow = narrow_sum(group, actives, columns).T
    keep, came, _ = of_widen
    came, grad_narrow, grad_adaptor, *head_grads = pin(
        came, grad_narrow, grad_adaptor, *head_grads
    )
    grad_widen = (keep[0].astype(jnp.float32) + came[0].astype(jnp.float32)).T
    return (grad_widen, grad_narrow, grad_adaptor, *head_grads)


def solution(mesh):
    placed = (
        P("dp", None),
        P(),
        P(None, "mp"),
        P("mp", None),
        P(),
        P(None, None, "mp"),
        P("mp", None),
        P("mp", None),
        P("mp", None),
        P(None, "dp", "mp"),
        P(None, "dp", "mp"),
        P(None, "dp", "mp"),
        P(),
        P(),
    )
    return jax.shard_map(
        local,
        mesh=mesh,
        in_specs=placed,
        out_specs=(
            P("mp", "dp"),
            P("mp", "dp"),
            P(None, "dp", "mp"),
            P("mp", "dp"),
            P("mp", "dp"),
            P("mp", "dp"),
        ),
        check_vma=False,
    )
```

```python
import functools

import jax
import jax.numpy as jnp
from jax import lax
from jax.experimental import pallas as pl
from jax.experimental.pallas import tpu as pltpu
from jax.sharding import PartitionSpec as P

PATCH = 32


slope_coef = 0.7978845608028654
cubic_coef = 0.044715


def smooth(value):
    return 0.5 * value * (1.0 + jnp.tanh(slope_coef * (value + cubic_coef * value * value * value)))


def smooth_slope(value):
    tangent = jnp.tanh(slope_coef * (value + cubic_coef * value * value * value))
    return 0.5 * (1.0 + tangent) + 0.5 * value * (1.0 - tangent * tangent) * slope_coef * (
        1.0 + 3.0 * cubic_coef * value * value
    )


def normalize(value, gain):
    centre = value - jnp.mean(value, axis=-1, keepdims=True)
    inverse = lax.rsqrt(jnp.mean(centre * centre, axis=-1, keepdims=True) + 1e-06)
    normal = centre * inverse
    return (normal * gain, normal, inverse)


def normalize_back(upstream, gain, normal, inverse):
    scaled = upstream * gain
    return inverse * (
        scaled
        - jnp.mean(scaled, axis=-1, keepdims=True)
        - normal * jnp.mean(scaled * normal, axis=-1, keepdims=True)
    )


def finish(product, square_student, square_target, student, target):
    joint = lax.rsqrt(square_student * square_target)
    cosine = product * joint
    slope = cosine[:, None] * student / square_student[:, None] - target * joint[:, None]
    return (cosine, slope)


def swap(value, axis, offset):
    count = lax.axis_size(axis)
    return lax.ppermute(value, axis, [(i, i ^ offset) for i in range(count)])


def ordered(value, count, position):
    cut = value.reshape((count, value.shape[0] // count) + value.shape[1:])
    return [
        lax.dynamic_index_in_dim(cut, position ^ j, 0, keepdims=False) for j in range(count)
    ]


def gather(piece, axis):
    return jnp.concatenate(
        [piece] + [swap(piece, axis, j) for j in range(1, lax.axis_size(axis))], axis=0
    )


def bits_of(count, low_first):
    bits = [1 << k for k in range(count.bit_length() - 1)]
    return bits if low_first else bits[::-1]


def scatter_begin(blocks, axis, low_first):
    bits = bits_of(len(blocks), low_first)
    leaving = [j for j in range(len(blocks)) if j & bits[0]]
    packed = jnp.concatenate([blocks[j].astype(jnp.bfloat16) for j in leaving], axis=0)
    held = {j: blocks[j] for j in range(len(blocks)) if j not in leaving}
    return [held, leaving, swap(packed, axis, bits[0])]


def scatter_rest(held, leaving, packed, axis, low_first):
    size = held[0].shape[0]
    bits = bits_of(lax.axis_size(axis), low_first)
    for bit, later in zip(bits, bits[1:]):
        for k, j in enumerate(leaving):
            piece = packed[k * size : (k + 1) * size]
            held[j ^ bit] = held[j ^ bit] + piece.astype(jnp.float32)
        leaving = [j for j in sorted(held) if j & later]
        packed = jnp.concatenate([held.pop(j).astype(jnp.bfloat16) for j in leaving], axis=0)
        packed = swap(packed, axis, later)
    return [held[0], packed]


def gather_doubling(piece, axis, low_first):
    held = {0: piece}
    size = piece.shape[0]
    for bit in bits_of(lax.axis_size(axis), low_first):
        order = sorted(held)
        packed = held[0] if len(order) == 1 else jnp.concatenate([held[j] for j in order], axis=0)
        packed = swap(packed, axis, bit)
        for k, j in enumerate(order):
            held[j ^ bit] = packed[k * size : (k + 1) * size]
    return jnp.concatenate([held[j] for j in sorted(held)], axis=0)


def reverse_bits(value, count):
    result = 0
    for k in range(count.bit_length() - 1):
        result = result * 2 + (value >> k) % 2
    return result


def limits(flops=0):
    return dict(
        compiler_params=pltpu.CompilerParams(vmem_limit_bytes=48 * 2**20),
        cost_estimate=pl.CostEstimate(flops=flops, bytes_accessed=0, transcendentals=0),
    )


IN_VMEM = pl.BlockSpec(memory_space=pltpu.VMEM)
IN_SMEM = pl.BlockSpec(memory_space=pltpu.SMEM)
IN_PLACE = pl.BlockSpec(memory_space=pl.ANY)


def pack_kernel(groups, images, turned, lag_ref, slot_ref, group_ref, *refs):
    count = len(turned)
    teachers, (keep_ref, send_ref) = refs[:count], refs[count : count + 2]
    held, sems = refs[count + 2 : -1], refs[-1]
    share = images // groups
    group = group_ref[0]
    copies = [
        pltpu.make_async_copy(teachers[t].at[lag_ref[t] - 1], held[t], sems.at[t])
        for t in range(count)
    ]
    for copy in copies:
        copy.start()
    slots = [slot_ref[group * images + i] for i in range(images)]
    places = []
    for i in range(images):
        rank = sum((slots[j] < slots[i]).astype(jnp.int32) for j in range(images) if j != i)
        away = lax.div(slots[i], images) ^ group
        spot = (away >> 1) * share + lax.rem(rank, share)
        places.append((away & 1, pl.ds(pl.multiple_of(spot * PATCH, PATCH), PATCH)))
    start = 0
    for t in range(count):
        copies[t].wait()
        value = held[t][...]
        if turned[t]:
            value = value.T
        columns = slice(start, start + value.shape[1])
        start += value.shape[1]
        for i, (side, to) in enumerate(places):
            piece = value[i * PATCH : (i + 1) * PATCH, :]

            @pl.when(side == 0)
            def _(piece=piece, to=to, columns=columns):
                keep_ref[to, columns] = piece

            @pl.when(side != 0)
            def _(piece=piece, to=to, columns=columns):
                send_ref[to, columns] = piece


def pack(step_lags, owner_slot, group, teachers, groups, images):
    rows = images * PATCH
    width = sum(teacher.shape[-1] for teacher in teachers)
    turned = [teacher.shape[-1] % 128 != 0 for teacher in teachers]
    teachers = [
        jnp.swapaxes(teacher, 1, 2) if turn else teacher for teacher, turn in zip(teachers, turned)
    ]
    half = jax.ShapeDtypeStruct((rows // 2, width), jnp.bfloat16)
    return pl.pallas_call(
        functools.partial(pack_kernel, groups, images, turned),
        out_shape=(half, half),
        in_specs=[IN_SMEM] * 3 + [IN_PLACE] * len(teachers),
        out_specs=(IN_VMEM, IN_VMEM),
        scratch_shapes=[pltpu.VMEM(teacher.shape[1:], jnp.bfloat16) for teacher in teachers]
        + [pltpu.SemaphoreType.DMA((len(teachers),))],
        name="pack",
        **limits(),
    )(step_lags, owner_slot, group.reshape(1), *teachers)


def place_kernel(images, place_ref, *refs):
    out_ref = refs[-1]
    each = images // (len(refs) - 1)
    for a in range(images):
        to = pl.ds(pl.multiple_of(place_ref[a] * PATCH, PATCH), PATCH)
        k = a % each
        out_ref[to, :] = refs[a // each][k * PATCH : (k + 1) * PATCH, :]


def loss_kernel(start, width, count, member_ref, *refs):
    parts, terms = refs[:count], refs[count:]
    sides = len(terms) // 3
    terms, slope_refs = terms[: 2 * sides], terms[2 * sides :]
    member = member_ref[0]
    pieces = [part[:, start : start + width].astype(jnp.float32) for part in parts]
    for bit in bits_of(count, True):
        flipped = (member & bit) != 0
        pieces = [jnp.where(flipped, pieces[j ^ bit], pieces[j]) for j in range(count)]
    target = jnp.concatenate(pieces, axis=-1)
    student = [
        terms[2 * k][...] + terms[2 * k + 1][...].astype(jnp.float32) for k in range(sides)
    ]
    student = student[0] if sides == 1 else jnp.concatenate(student, axis=-1)
    product = jnp.sum(student * target, axis=-1, keepdims=True)
    square_student = jnp.sum(student * student, axis=-1, keepdims=True) + 1e-06
    square_target = jnp.sum(target * target, axis=-1, keepdims=True) + 1e-06
    joint = lax.rsqrt(square_student * square_target)
    cosine = product * joint
    slope = ((cosine / square_student) * student - target * joint).astype(jnp.bfloat16)
    wide = slope.shape[1] // sides
    for k in range(sides):
        slope_refs[k][...] = slope[:, k * wide : (k + 1) * wide]


def loss(member, terms, parts, start, width):
    flat = [value for pair in terms for value in pair]
    return pl.pallas_call(
        functools.partial(loss_kernel, start, width, len(parts)),
        out_shape=[jax.ShapeDtypeStruct(last.shape, jnp.bfloat16) for _, last in terms],
        in_specs=[IN_SMEM] + [IN_VMEM] * (len(parts) + len(flat)),
        out_specs=[IN_VMEM] * len(terms),
        name="loss",
        **limits(),
    )(member.reshape(1), *parts, *flat)


def beside(refs):
    return refs[0][...] if len(refs) == 1 else jnp.concatenate([r[...] for r in refs], axis=1)


def product_kernel(groups, shape, spot_ref, *refs):
    keep_ref, send_ref = refs[-2:]
    side, base = spot_ref[0] != 0, spot_ref[1]
    tall = keep_ref.shape[1]
    used = column = 0
    for lefts, rights in shape:
        left = beside(refs[used : used + lefts])
        right = beside(refs[used + lefts : used + lefts + rights])
        used += lefts + rights
        cut, wide = left.shape[1] // groups, right.shape[1]
        columns = slice(column, column + wide)
        column += wide
        full = lax.dot_general(
            left, right, (((0,), (0,)), ((), ())), preferred_element_type=jnp.float32
        )
        for pair in range(groups // 2):
            even = full[2 * pair * cut : (2 * pair + 1) * cut, :]
            odd = full[(2 * pair + 1) * cut : (2 * pair + 2) * cut, :]
            at = base ^ reverse_bits(pair, groups // 2)
            if cut < tall:
                rest = jnp.zeros((tall - cut, wide), jnp.float32)
                even = jnp.concatenate([even, rest], axis=0)
                odd = jnp.concatenate([odd, rest], axis=0)
            keep_ref[at, :, columns] = jnp.where(side, odd, even).astype(jnp.bfloat16)
            send_ref[at, :, columns] = jnp.where(side, even, odd).astype(jnp.bfloat16)


def product(pairs, groups, group, flops=0):
    talls = [sum(left.shape[1] for left in lefts) for lefts, _ in pairs]
    wides = [sum(right.shape[1] for right in rights) for _, rights in pairs]
    tall, wide = max(talls) // groups, sum(wides)
    half = jax.ShapeDtypeStruct((groups // 2, tall, wide), jnp.bfloat16)
    spot = jnp.stack([group % 2, reverse_bits(group // 2, groups // 2)]).astype(jnp.int32)
    flat = [value for lefts, rights in pairs for value in (*lefts, *rights)]
    return pl.pallas_call(
        functools.partial(product_kernel, groups, [(len(l), len(r)) for l, r in pairs]),
        out_shape=(half, half),
        in_specs=[IN_SMEM] + [IN_VMEM] * len(flat),
        out_specs=(IN_VMEM, IN_VMEM),
        name="product",
        **limits(flops),
    )(spot, *flat)


def narrow_kernel(count, group_ref, active_ref, *refs):
    out_ref = refs[-1]
    columns = jnp.concatenate([ref[0] for ref in refs[:count]], axis=1)
    term = jnp.dot(columns, active_ref[0], preferred_element_type=jnp.float32)

    @pl.when(pl.program_id(0) == 0)
    def _():
        out_ref[...] = term

    @pl.when(pl.program_id(0) != 0)
    def _():
        out_ref[...] += term


def narrow_sum(group, actives, columns):
    groups, rows, units = actives.shape
    cut = columns[0].shape[1]
    return pl.pallas_call(
        functools.partial(narrow_kernel, len(columns)),
        out_shape=jax.ShapeDtypeStruct((cut, units), jnp.float32),
        grid_spec=pltpu.PrefetchScalarGridSpec(
            num_scalar_prefetch=1,
            grid=(groups,),
            in_specs=[pl.BlockSpec((1, rows, units), lambda o, g: (o ^ g[0], 0, 0))]
            + [pl.BlockSpec((1, cut, column.shape[2]), lambda o, g: (o, 0, 0)) for column in columns],
            out_specs=pl.BlockSpec((cut, units), lambda o, g: (0, 0)),
        ),
        name="narrow",
        **limits(2**35),
    )(group.reshape(1), actives, *columns)


def pin(*values):
    return lax.optimization_barrier(values)


def merge_kernel(held_ref, came_ref, kept_ref, sent_ref):
    half = kept_ref.shape[0]
    for k in range(half):
        low = held_ref[k].astype(jnp.float32) + came_ref[k].astype(jnp.float32)
        high = held_ref[half + k].astype(jnp.float32) + came_ref[half + k].astype(jnp.float32)
        kept_ref[k] = low
        sent_ref[k] = high.astype(jnp.bfloat16)


def merge(held, came):
    shape = (held.shape[0] // 2, *held.shape[1:])
    return pl.pallas_call(
        merge_kernel,
        out_shape=(
            jax.ShapeDtypeStruct(shape, jnp.float32),
            jax.ShapeDtypeStruct(shape, jnp.bfloat16),
        ),
        in_specs=[IN_VMEM, IN_VMEM],
        out_specs=(IN_VMEM, IN_VMEM),
        name="merge",
        **limits(2**35),
    )(held, came)


def begin(halves):
    keep, send = halves
    bits = bits_of(2 * keep.shape[0], True)[1:]
    return (keep, swap(send, "dp", 1), bits)


def advance(state, kernel=False):
    keep, came, bits = state
    if not bits:
        return state
    if kernel:
        kept, sent = merge(keep, came)
    else:
        held = keep.astype(jnp.float32) + came.astype(jnp.float32)
        half = held.shape[0] // 2
        kept, sent = held[:half], held[half:].astype(jnp.bfloat16)
    return (kept, swap(sent, "dp", bits[0]), bits[1:])


def finish_kernel(cuts, *refs):
    count = len(cuts)
    outs = refs[2 * count :]
    used = 0
    for k in range(count):
        total = refs[2 * k][0].astype(jnp.float32) + refs[2 * k + 1][0].astype(jnp.float32)
        for rows, start, end in cuts[k]:
            outs[used][...] = total[:rows, start:end]
            used += 1


def finish(states, cuts):
    for state in states:
        assert not state[2]
    return pl.pallas_call(
        functools.partial(finish_kernel, cuts),
        out_shape=[
            jax.ShapeDtypeStruct((rows, end - start), jnp.float32)
            for cut in cuts
            for rows, start, end in cut
        ],
        in_specs=[IN_VMEM] * (2 * len(states)),
        out_specs=[IN_VMEM] * sum(len(cut) for cut in cuts),
        name="finish",
        **limits(2**35),
    )(*[value for state in states for value in state[:2]])


def settle(state, kernel=False):
    while state[2]:
        state = advance(state, kernel)
    return state


def arrive(state, came):
    return (state[0], came, state[2])


def local(
    tokens,
    norm_gain,
    widen_weight,
    narrow_weight,
    final_gain,
    adaptor_in,
    head_dino,
    head_siglip,
    head_sam,
    teacher_dino,
    teacher_siglip,
    teacher_sam,
    step_lags,
    owner_slot,
):
    groups = lax.axis_size("dp")
    members = lax.axis_size("mp")
    group = lax.axis_index("dp")
    member = lax.axis_index("mp")
    rows = tokens.shape[0]
    images = rows // PATCH
    share = images // groups
    block = rows // members
    heads = (head_dino, head_siglip, head_sam)
    teachers = (teacher_dino, teacher_siglip, teacher_sam)
    widths = [teacher.shape[-1] for teacher in teachers]
    exact = dict(preferred_element_type=jnp.float32)

    slots = owner_slot.reshape(groups, images)
    rank = jnp.sum(slots[:, :, None] > slots[:, None, :], axis=2, dtype=jnp.int32) % share
    source = lax.broadcasted_iota(jnp.int32, (groups, images), 0)
    landing = (source ^ group) * share + rank
    slot_rows = group * images + lax.broadcasted_iota(jnp.int32, (images,), 0)
    found = slots.reshape(1, -1) == slot_rows[:, None]
    landed = jnp.sum(jnp.where(found, landing.reshape(1, -1), 0), axis=1)
    position = lax.broadcasted_iota(jnp.int32, (images,), 0) ^ (member * (images // members))
    at = lax.broadcasted_iota(jnp.int32, (images, images), 0)
    place = jnp.sum(jnp.where(landed[None, :] == at, position[None, :], 0), axis=1)

    tokens = jnp.concatenate(ordered(tokens, members, member), axis=0)
    first, _, _ = normalize(tokens.astype(jnp.float32), norm_gain)
    first = lax.optimization_barrier(first.astype(jnp.bfloat16))
    widened = jnp.dot(first, widen_weight, **exact)
    active = smooth(widened).astype(jnp.bfloat16)
    mixed = jnp.dot(active, narrow_weight, **exact).reshape(members, block, -1)
    mixed, step_lags = pin(mixed, step_lags)
    came = [swap(mixed[j].astype(jnp.bfloat16), "mp", j) for j in range(1, members)]
    kept, crossing = pack(step_lags, owner_slot, group, teachers, groups, images)
    came[0], crossing = pin(came[0], swap(crossing, "dp", 1))
    hidden = tokens[:block].astype(jnp.float32) + mixed[0]
    for piece in came:
        hidden = hidden + piece.astype(jnp.float32)
    pairs = jnp.stack(
        [
            kept.reshape(groups // 2, share * PATCH, -1),
            crossing.reshape(groups // 2, share * PATCH, -1),
        ],
        axis=1,
    ).reshape(groups // 2, 2 * share * PATCH, -1)
    arrived = [pairs[0]] + [swap(pairs[o], "dp", 2 * o) for o in range(1, groups // 2)]
    owned = pl.pallas_call(
        functools.partial(place_kernel, images),
        out_shape=jax.ShapeDtypeStruct((rows, sum(widths)), jnp.bfloat16),
        in_specs=[IN_SMEM] + [IN_VMEM] * len(arrived),
        out_specs=IN_VMEM,
        name="place",
        **limits(),
    )(place, *arrived)

    final_rows, normal_rows, inverse_rows = normalize(hidden, final_gain)
    final = gather(final_rows.astype(jnp.bfloat16), "mp")
    bend_two = smooth_slope(widened)
    final, late, own, bend_two = pin(final, active, owned[:block], bend_two)
    actives = lax.all_gather(late, "dp")

    owned = owned.reshape(members, block, -1)
    parts = [own] + [swap(owned[j], "mp", j) for j in range(1, members)]

    ways = ((True, False), (True,), (False,))
    befores, lifteds, students = [], [], []
    for index in range(3):
        before = jnp.dot(final, adaptor_in[index], **exact)
        lifted = smooth(before).astype(jnp.bfloat16)
        partial = jnp.dot(lifted, heads[index], **exact).reshape(members, block, -1)
        if index < 2:
            final, partial = pin(final, partial)
        befores.append(before)
        lifteds.append(lifted)
        wide = partial.shape[-1] // len(ways[index])
        students.append(
            [
                scatter_begin(list(partial[:, :, k * wide : (k + 1) * wide]), "mp", way)
                for k, way in enumerate(ways[index])
            ]
        )
    students[0][0][2], parts[0] = pin(students[0][0][2], parts[0])
    students = [
        [scatter_rest(*term, "mp", way) for term, way in zip(terms, ways[index])]
        for index, terms in enumerate(students)
    ]
    bends = [smooth_slope(before) for before in befores]
    students[0][0][1], *bends = pin(students[0][0][1], *bends)
    slopes = []
    start = 0
    for index in range(3):
        made = loss(member, students[index], parts, start, widths[index])
        start += widths[index]
        slopes.append([gather_doubling(s, "mp", way) for s, way in zip(made, ways[index])])
    inners = []
    upstream = 0.0
    for index in range(3):
        back = 0.0
        wide = slopes[index][0].shape[1]
        for k, slope in enumerate(slopes[index]):
            head = heads[index][:, k * wide : (k + 1) * wide]
            back = back + jnp.einsum("rc,hc->rh", slope, head, **exact)
        inner = (back * bends[index]).astype(jnp.bfloat16)
        inners.append(inner)
        upstream = upstream + jnp.einsum("rh,dh->rd", inner, adaptor_in[index], **exact)
        if index == 1:
            pairs = [(slopes[k], lifteds[k : k + 1]) for k in range(2)]
            of_heads = begin(product(pairs, groups, group))
            slopes[2][0], arrived = pin(slopes[2][0], of_heads[1])
            of_heads = advance(arrive(of_heads, arrived))
    upstream = upstream.reshape(members, block, -1)
    came = [swap(upstream[j].astype(jnp.bfloat16), "mp", j) for j in range(1, members)]

    mine, *inners = pin(upstream[0], *inners)
    of_rest = begin(
        product([([final], inners), (slopes[2], lifteds[2:])], groups, group)
    )
    came[0], one, two = pin(came[0], of_heads[1], of_rest[1])
    of_heads = arrive(of_heads, one)
    of_rest = advance(arrive(of_rest, two))
    total = mine
    for piece in came:
        total = total + piece.astype(jnp.float32)
    through_rows = normalize_back(total, final_gain, normal_rows, inverse_rows)
    through_rows = through_rows.astype(jnp.bfloat16)
    came = [swap(through_rows, "mp", j) for j in range(1, members)]
    turned = through_rows.T.reshape(groups, -1, block)
    turned = [lax.dynamic_index_in_dim(turned, group ^ o, 0) for o in range(groups)]
    odd = swap(jnp.concatenate(turned[1::2], axis=0), "dp", 1)
    came[-1], odd, one, two, actives = pin(came[-1], odd, of_heads[1], of_rest[1], actives)
    of_heads, of_rest = arrive(of_heads, one), arrive(of_rest, two)
    through = jnp.concatenate([through_rows, *came], axis=0)
    both = [jnp.concatenate([turned[2 * o], odd[o : o + 1]]) for o in range(groups // 2)]
    both = [both[0]] + [swap(both[o], "dp", 2 * o) for o in range(1, groups // 2)]

    back_two = jnp.einsum("rd,fd->rf", through, narrow_weight, **exact)
    inner_two = (back_two * bend_two).astype(jnp.bfloat16)
    inner_two, one, two = pin(inner_two, of_heads[1], of_rest[1])
    of_heads, of_rest = settle(arrive(of_heads, one)), settle(arrive(of_rest, two))
    of_widen = begin(product([([first], [inner_two])], groups, group, 2**35))
    of_widen = advance(of_widen, True)
    keep, *both = pin(of_widen[0], *both)
    of_widen = (keep, *of_widen[1:])
    columns = jnp.concatenate(both, axis=0)
    columns = [columns] + [swap(columns, "mp", j) for j in range(1, members)]
    of_heads, of_rest = settle(of_heads), settle(of_rest)
    while of_widen[2]:
        one, two, *columns[1:] = pin(of_widen[1], of_rest[1], *columns[1:])
        of_widen, of_rest = arrive(of_widen, one), arrive(of_rest, two)
        of_widen = advance(of_widen, True)
    wide = lifteds[0].shape[1]
    cuts = [head.shape[1] // groups for head in heads]
    deep = final.shape[1] // groups
    spans = [(k * wide, (k + 1) * wide) for k in range(4)]
    made = finish(
        [of_heads, of_rest],
        [
            [(cuts[0], *spans[0]), (cuts[1], *spans[1])],
            [(deep, *span) for span in spans[:3]] + [(cuts[2], *spans[3])],
        ],
    )
    head_grads = [made[0].T, made[1].T, made[5].T]
    grad_adaptor = jnp.stack(made[2:5])
    grad_narrow = narrow_sum(group, actives, columns).T
    keep, came, _ = of_widen
    came, grad_narrow, grad_adaptor, *head_grads = pin(
        came, grad_narrow, grad_adaptor, *head_grads
    )
    grad_widen = (keep[0].astype(jnp.float32) + came[0].astype(jnp.float32)).T
    return (grad_widen, grad_narrow, grad_adaptor, *head_grads)


def solution(mesh):
    placed = (
        P("dp", None),
        P(),
        P(None, "mp"),
        P("mp", None),
        P(),
        P(None, None, "mp"),
        P("mp", None),
        P("mp", None),
        P("mp", None),
        P(None, "dp", "mp"),
        P(None, "dp", "mp"),
        P(None, "dp", "mp"),
        P(),
        P(),
    )
    return jax.shard_map(
        local,
        mesh=mesh,
        in_specs=placed,
        out_specs=(
            P("mp", "dp"),
            P("mp", "dp"),
            P(None, "dp", "mp"),
            P("mp", "dp"),
            P("mp", "dp"),
            P("mp", "dp"),
        ),
        check_vma=False,
    )
```

```python
import functools

import jax
import jax.numpy as jnp
from jax import lax
from jax.experimental import pallas as pl
from jax.experimental.pallas import tpu as pltpu
from jax.sharding import PartitionSpec as P

PATCH = 32


slope_coef = 0.7978845608028654
cubic_coef = 0.044715


def smooth(value):
    return 0.5 * value * (1.0 + jnp.tanh(slope_coef * (value + cubic_coef * value * value * value)))


def smooth_slope(value):
    tangent = jnp.tanh(slope_coef * (value + cubic_coef * value * value * value))
    return 0.5 * (1.0 + tangent) + 0.5 * value * (1.0 - tangent * tangent) * slope_coef * (
        1.0 + 3.0 * cubic_coef * value * value
    )


def normalize(value, gain):
    centre = value - jnp.mean(value, axis=-1, keepdims=True)
    inverse = lax.rsqrt(jnp.mean(centre * centre, axis=-1, keepdims=True) + 1e-06)
    normal = centre * inverse
    return (normal * gain, normal, inverse)


def normalize_back(upstream, gain, normal, inverse):
    scaled = upstream * gain
    return inverse * (
        scaled
        - jnp.mean(scaled, axis=-1, keepdims=True)
        - normal * jnp.mean(scaled * normal, axis=-1, keepdims=True)
    )


def finish(product, square_student, square_target, student, target):
    joint = lax.rsqrt(square_student * square_target)
    cosine = product * joint
    slope = cosine[:, None] * student / square_student[:, None] - target * joint[:, None]
    return (cosine, slope)


def swap(value, axis, offset):
    count = lax.axis_size(axis)
    return lax.ppermute(value, axis, [(i, i ^ offset) for i in range(count)])


def ordered(value, count, position):
    cut = value.reshape((count, value.shape[0] // count) + value.shape[1:])
    return [
        lax.dynamic_index_in_dim(cut, position ^ j, 0, keepdims=False) for j in range(count)
    ]


def gather(piece, axis):
    return jnp.concatenate(
        [piece] + [swap(piece, axis, j) for j in range(1, lax.axis_size(axis))], axis=0
    )


def bits_of(count, low_first):
    bits = [1 << k for k in range(count.bit_length() - 1)]
    return bits if low_first else bits[::-1]


def scatter_begin(blocks, axis, low_first):
    bits = bits_of(len(blocks), low_first)
    leaving = [j for j in range(len(blocks)) if j & bits[0]]
    packed = jnp.concatenate([blocks[j].astype(jnp.bfloat16) for j in leaving], axis=0)
    held = {j: blocks[j] for j in range(len(blocks)) if j not in leaving}
    return [held, leaving, swap(packed, axis, bits[0])]


def scatter_rest(held, leaving, packed, axis, low_first):
    size = held[0].shape[0]
    bits = bits_of(lax.axis_size(axis), low_first)
    for bit, later in zip(bits, bits[1:]):
        for k, j in enumerate(leaving):
            piece = packed[k * size : (k + 1) * size]
            held[j ^ bit] = held[j ^ bit] + piece.astype(jnp.float32)
        leaving = [j for j in sorted(held) if j & later]
        packed = jnp.concatenate([held.pop(j).astype(jnp.bfloat16) for j in leaving], axis=0)
        packed = swap(packed, axis, later)
    return [held[0], packed]


def gather_doubling(piece, axis, low_first):
    held = {0: piece}
    size = piece.shape[0]
    for bit in bits_of(lax.axis_size(axis), low_first):
        order = sorted(held)
        packed = held[0] if len(order) == 1 else jnp.concatenate([held[j] for j in order], axis=0)
        packed = swap(packed, axis, bit)
        for k, j in enumerate(order):
            held[j ^ bit] = packed[k * size : (k + 1) * size]
    return jnp.concatenate([held[j] for j in sorted(held)], axis=0)


def reverse_bits(value, count):
    result = 0
    for k in range(count.bit_length() - 1):
        result = result * 2 + (value >> k) % 2
    return result


def limits(flops=0):
    return dict(
        compiler_params=pltpu.CompilerParams(vmem_limit_bytes=48 * 2**20),
        cost_estimate=pl.CostEstimate(flops=flops, bytes_accessed=0, transcendentals=0),
    )


IN_VMEM = pl.BlockSpec(memory_space=pltpu.VMEM)
IN_SMEM = pl.BlockSpec(memory_space=pltpu.SMEM)
IN_PLACE = pl.BlockSpec(memory_space=pl.ANY)


def pack_kernel(groups, images, turned, lag_ref, slot_ref, group_ref, *refs):
    count = len(turned)
    teachers, (keep_ref, send_ref) = refs[:count], refs[count : count + 2]
    held, sems = refs[count + 2 : -1], refs[-1]
    share = images // groups
    group = group_ref[0]
    copies = [
        pltpu.make_async_copy(teachers[t].at[lag_ref[t] - 1], held[t], sems.at[t])
        for t in range(count)
    ]
    for copy in copies:
        copy.start()
    slots = [slot_ref[group * images + i] for i in range(images)]
    places = []
    for i in range(images):
        rank = sum((slots[j] < slots[i]).astype(jnp.int32) for j in range(images) if j != i)
        away = lax.div(slots[i], images) ^ group
        spot = (away >> 1) * share + lax.rem(rank, share)
        places.append((away & 1, pl.ds(pl.multiple_of(spot * PATCH, PATCH), PATCH)))
    start = 0
    for t in range(count):
        copies[t].wait()
        value = held[t][...]
        if turned[t]:
            value = value.T
        columns = slice(start, start + value.shape[1])
        start += value.shape[1]
        for i, (side, to) in enumerate(places):
            piece = value[i * PATCH : (i + 1) * PATCH, :]

            @pl.when(side == 0)
            def _(piece=piece, to=to, columns=columns):
                keep_ref[to, columns] = piece

            @pl.when(side != 0)
            def _(piece=piece, to=to, columns=columns):
                send_ref[to, columns] = piece


def pack(step_lags, owner_slot, group, teachers, groups, images):
    rows = images * PATCH
    width = sum(teacher.shape[-1] for teacher in teachers)
    turned = [teacher.shape[-1] % 128 != 0 for teacher in teachers]
    teachers = [
        jnp.swapaxes(teacher, 1, 2) if turn else teacher for teacher, turn in zip(teachers, turned)
    ]
    half = jax.ShapeDtypeStruct((rows // 2, width), jnp.bfloat16)
    return pl.pallas_call(
        functools.partial(pack_kernel, groups, images, turned),
        out_shape=(half, half),
        in_specs=[IN_SMEM] * 3 + [IN_PLACE] * len(teachers),
        out_specs=(IN_VMEM, IN_VMEM),
        scratch_shapes=[pltpu.VMEM(teacher.shape[1:], jnp.bfloat16) for teacher in teachers]
        + [pltpu.SemaphoreType.DMA((len(teachers),))],
        name="pack",
        **limits(),
    )(step_lags, owner_slot, group.reshape(1), *teachers)


def place_kernel(images, place_ref, *refs):
    out_ref = refs[-1]
    each = images // (len(refs) - 1)
    for a in range(images):
        to = pl.ds(pl.multiple_of(place_ref[a] * PATCH, PATCH), PATCH)
        k = a % each
        out_ref[to, :] = refs[a // each][k * PATCH : (k + 1) * PATCH, :]


def loss_kernel(start, width, count, member_ref, *refs):
    parts, terms = refs[:count], refs[count:]
    sides = len(terms) // 3
    terms, slope_refs = terms[: 2 * sides], terms[2 * sides :]
    member = member_ref[0]
    pieces = [part[:, start : start + width].astype(jnp.float32) for part in parts]
    for bit in bits_of(count, True):
        flipped = (member & bit) != 0
        pieces = [jnp.where(flipped, pieces[j ^ bit], pieces[j]) for j in range(count)]
    target = jnp.concatenate(pieces, axis=-1)
    student = [
        terms[2 * k][...] + terms[2 * k + 1][...].astype(jnp.float32) for k in range(sides)
    ]
    student = student[0] if sides == 1 else jnp.concatenate(student, axis=-1)
    product = jnp.sum(student * target, axis=-1, keepdims=True)
    square_student = jnp.sum(student * student, axis=-1, keepdims=True) + 1e-06
    square_target = jnp.sum(target * target, axis=-1, keepdims=True) + 1e-06
    joint = lax.rsqrt(square_student * square_target)
    cosine = product * joint
    slope = ((cosine / square_student) * student - target * joint).astype(jnp.bfloat16)
    wide = slope.shape[1] // sides
    for k in range(sides):
        slope_refs[k][...] = slope[:, k * wide : (k + 1) * wide]


def loss(member, terms, parts, start, width):
    flat = [value for pair in terms for value in pair]
    return pl.pallas_call(
        functools.partial(loss_kernel, start, width, len(parts)),
        out_shape=[jax.ShapeDtypeStruct(last.shape, jnp.bfloat16) for _, last in terms],
        in_specs=[IN_SMEM] + [IN_VMEM] * (len(parts) + len(flat)),
        out_specs=[IN_VMEM] * len(terms),
        name="loss",
        **limits(),
    )(member.reshape(1), *parts, *flat)


def beside(refs):
    return refs[0][...] if len(refs) == 1 else jnp.concatenate([r[...] for r in refs], axis=1)


def product_kernel(groups, shape, spot_ref, *refs):
    keep_ref, send_ref = refs[-2:]
    side, base = spot_ref[0] != 0, spot_ref[1]
    tall = keep_ref.shape[1]
    used = column = 0
    for lefts, rights in shape:
        left = beside(refs[used : used + lefts])
        right = beside(refs[used + lefts : used + lefts + rights])
        used += lefts + rights
        cut, wide = left.shape[1] // groups, right.shape[1]
        columns = slice(column, column + wide)
        column += wide
        full = lax.dot_general(
            left, right, (((0,), (0,)), ((), ())), preferred_element_type=jnp.float32
        )
        for pair in range(groups // 2):
            even = full[2 * pair * cut : (2 * pair + 1) * cut, :]
            odd = full[(2 * pair + 1) * cut : (2 * pair + 2) * cut, :]
            at = base ^ reverse_bits(pair, groups // 2)
            if cut < tall:
                rest = jnp.zeros((tall - cut, wide), jnp.float32)
                even = jnp.concatenate([even, rest], axis=0)
                odd = jnp.concatenate([odd, rest], axis=0)
            keep_ref[at, :, columns] = jnp.where(side, odd, even).astype(jnp.bfloat16)
            send_ref[at, :, columns] = jnp.where(side, even, odd).astype(jnp.bfloat16)


def product(pairs, groups, group, flops=0):
    talls = [sum(left.shape[1] for left in lefts) for lefts, _ in pairs]
    wides = [sum(right.shape[1] for right in rights) for _, rights in pairs]
    tall, wide = max(talls) // groups, sum(wides)
    half = jax.ShapeDtypeStruct((groups // 2, tall, wide), jnp.bfloat16)
    spot = jnp.stack([group % 2, reverse_bits(group // 2, groups // 2)]).astype(jnp.int32)
    flat = [value for lefts, rights in pairs for value in (*lefts, *rights)]
    return pl.pallas_call(
        functools.partial(product_kernel, groups, [(len(l), len(r)) for l, r in pairs]),
        out_shape=(half, half),
        in_specs=[IN_SMEM] + [IN_VMEM] * len(flat),
        out_specs=(IN_VMEM, IN_VMEM),
        name="product",
        **limits(flops),
    )(spot, *flat)


def narrow_kernel(count, group_ref, active_ref, *refs):
    out_ref = refs[-1]
    columns = jnp.concatenate([ref[0] for ref in refs[:count]], axis=1)
    term = jnp.dot(columns, active_ref[0], preferred_element_type=jnp.float32)

    @pl.when(pl.program_id(0) == 0)
    def _():
        out_ref[...] = term

    @pl.when(pl.program_id(0) != 0)
    def _():
        out_ref[...] += term


def narrow_sum(group, actives, columns):
    groups, rows, units = actives.shape
    cut = columns[0].shape[1]
    return pl.pallas_call(
        functools.partial(narrow_kernel, len(columns)),
        out_shape=jax.ShapeDtypeStruct((cut, units), jnp.float32),
        grid_spec=pltpu.PrefetchScalarGridSpec(
            num_scalar_prefetch=1,
            grid=(groups,),
            in_specs=[pl.BlockSpec((1, rows, units), lambda o, g: (o ^ g[0], 0, 0))]
            + [pl.BlockSpec((1, cut, column.shape[2]), lambda o, g: (o, 0, 0)) for column in columns],
            out_specs=pl.BlockSpec((cut, units), lambda o, g: (0, 0)),
        ),
        name="narrow",
        **limits(2**35),
    )(group.reshape(1), actives, *columns)


def pin(*values):
    return lax.optimization_barrier(values)


def merge_kernel(held_ref, came_ref, kept_ref, sent_ref):
    half = kept_ref.shape[0]
    for k in range(half):
        low = held_ref[k].astype(jnp.float32) + came_ref[k].astype(jnp.float32)
        high = held_ref[half + k].astype(jnp.float32) + came_ref[half + k].astype(jnp.float32)
        kept_ref[k] = low
        sent_ref[k] = high.astype(jnp.bfloat16)


def merge(held, came):
    shape = (held.shape[0] // 2, *held.shape[1:])
    return pl.pallas_call(
        merge_kernel,
        out_shape=(
            jax.ShapeDtypeStruct(shape, jnp.float32),
            jax.ShapeDtypeStruct(shape, jnp.bfloat16),
        ),
        in_specs=[IN_VMEM, IN_VMEM],
        out_specs=(IN_VMEM, IN_VMEM),
        name="merge",
        **limits(2**35),
    )(held, came)


def begin(halves):
    keep, send = halves
    bits = bits_of(2 * keep.shape[0], True)[1:]
    return (keep, swap(send, "dp", 1), bits)


def advance(state, kernel=False):
    keep, came, bits = state
    if not bits:
        return state
    if kernel:
        kept, sent = merge(keep, came)
    else:
        held = keep.astype(jnp.float32) + came.astype(jnp.float32)
        half = held.shape[0] // 2
        kept, sent = held[:half], held[half:].astype(jnp.bfloat16)
    return (kept, swap(sent, "dp", bits[0]), bits[1:])


def finish_kernel(cuts, *refs):
    count = len(cuts)
    outs = refs[2 * count :]
    used = 0
    for k in range(count):
        total = refs[2 * k][0].astype(jnp.float32) + refs[2 * k + 1][0].astype(jnp.float32)
        for rows, start, end in cuts[k]:
            outs[used][...] = total[:rows, start:end]
            used += 1


def finish(states, cuts):
    for state in states:
        assert not state[2]
    return pl.pallas_call(
        functools.partial(finish_kernel, cuts),
        out_shape=[
            jax.ShapeDtypeStruct((rows, end - start), jnp.float32)
            for cut in cuts
            for rows, start, end in cut
        ],
        in_specs=[IN_VMEM] * (2 * len(states)),
        out_specs=[IN_VMEM] * sum(len(cut) for cut in cuts),
        name="finish",
        **limits(2**35),
    )(*[value for state in states for value in state[:2]])


def settle(state, kernel=False):
    while state[2]:
        state = advance(state, kernel)
    return state


def arrive(state, came):
    return (state[0], came, state[2])


def local(
    tokens,
    norm_gain,
    widen_weight,
    narrow_weight,
    final_gain,
    adaptor_in,
    head_dino,
    head_siglip,
    head_sam,
    teacher_dino,
    teacher_siglip,
    teacher_sam,
    step_lags,
    owner_slot,
):
    groups = lax.axis_size("dp")
    members = lax.axis_size("mp")
    group = lax.axis_index("dp")
    member = lax.axis_index("mp")
    rows = tokens.shape[0]
    images = rows // PATCH
    share = images // groups
    block = rows // members
    heads = (head_dino, head_siglip, head_sam)
    teachers = (teacher_dino, teacher_siglip, teacher_sam)
    widths = [teacher.shape[-1] for teacher in teachers]
    exact = dict(preferred_element_type=jnp.float32)

    slots = owner_slot.reshape(groups, images)
    rank = jnp.sum(slots[:, :, None] > slots[:, None, :], axis=2, dtype=jnp.int32) % share
    source = lax.broadcasted_iota(jnp.int32, (groups, images), 0)
    landing = (source ^ group) * share + rank
    slot_rows = group * images + lax.broadcasted_iota(jnp.int32, (images,), 0)
    found = slots.reshape(1, -1) == slot_rows[:, None]
    landed = jnp.sum(jnp.where(found, landing.reshape(1, -1), 0), axis=1)
    position = lax.broadcasted_iota(jnp.int32, (images,), 0) ^ (member * (images // members))
    at = lax.broadcasted_iota(jnp.int32, (images, images), 0)
    place = jnp.sum(jnp.where(landed[None, :] == at, position[None, :], 0), axis=1)

    tokens = jnp.concatenate(ordered(tokens, members, member), axis=0)
    first, _, _ = normalize(tokens.astype(jnp.float32), norm_gain)
    first = lax.optimization_barrier(first.astype(jnp.bfloat16))
    widened = jnp.dot(first, widen_weight, **exact)
    active = smooth(widened).astype(jnp.bfloat16)
    mixed = jnp.dot(active, narrow_weight, **exact).reshape(members, block, -1)
    mixed, step_lags = pin(mixed, step_lags)
    came = [swap(mixed[j].astype(jnp.bfloat16), "mp", j) for j in range(1, members)]
    kept, crossing = pack(step_lags, owner_slot, group, teachers, groups, images)
    came[0], crossing = pin(came[0], swap(crossing, "dp", 1))
    hidden = tokens[:block].astype(jnp.float32) + mixed[0]
    for piece in came:
        hidden = hidden + piece.astype(jnp.float32)
    pairs = jnp.stack(
        [
            kept.reshape(groups // 2, share * PATCH, -1),
            crossing.reshape(groups // 2, share * PATCH, -1),
        ],
        axis=1,
    ).reshape(groups // 2, 2 * share * PATCH, -1)
    arrived = [pairs[0]] + [swap(pairs[o], "dp", 2 * o) for o in range(1, groups // 2)]
    owned = pl.pallas_call(
        functools.partial(place_kernel, images),
        out_shape=jax.ShapeDtypeStruct((rows, sum(widths)), jnp.bfloat16),
        in_specs=[IN_SMEM] + [IN_VMEM] * len(arrived),
        out_specs=IN_VMEM,
        name="place",
        **limits(),
    )(place, *arrived)

    final_rows, normal_rows, inverse_rows = normalize(hidden, final_gain)
    final = gather(final_rows.astype(jnp.bfloat16), "mp")
    bend_two = smooth_slope(widened)
    final, late, own, bend_two = pin(final, active, owned[:block], bend_two)
    actives = lax.all_gather(late, "dp")

    owned = owned.reshape(members, block, -1)
    parts = [own] + [swap(owned[j], "mp", j) for j in range(1, members)]

    ways = ((True, False), (True,), (False,))
    befores, lifteds, students = [], [], []
    for index in range(3):
        before = jnp.dot(final, adaptor_in[index], **exact)
        lifted = smooth(before).astype(jnp.bfloat16)
        partial = jnp.dot(lifted, heads[index], **exact).reshape(members, block, -1)
        if index < 2:
            final, partial = pin(final, partial)
        befores.append(before)
        lifteds.append(lifted)
        wide = partial.shape[-1] // len(ways[index])
        students.append(
            [
                scatter_begin(list(partial[:, :, k * wide : (k + 1) * wide]), "mp", way)
                for k, way in enumerate(ways[index])
            ]
        )
    students[0][0][2], parts[0] = pin(students[0][0][2], parts[0])
    students = [
        [scatter_rest(*term, "mp", way) for term, way in zip(terms, ways[index])]
        for index, terms in enumerate(students)
    ]
    bends = [smooth_slope(before) for before in befores]
    students[0][0][1], *bends = pin(students[0][0][1], *bends)
    slopes = []
    start = 0
    for index in range(3):
        made = loss(member, students[index], parts, start, widths[index])
        start += widths[index]
        slopes.append([gather_doubling(s, "mp", way) for s, way in zip(made, ways[index])])
    inners = []
    upstream = 0.0
    for index in range(3):
        back = 0.0
        wide = slopes[index][0].shape[1]
        for k, slope in enumerate(slopes[index]):
            head = heads[index][:, k * wide : (k + 1) * wide]
            back = back + jnp.einsum("rc,hc->rh", slope, head, **exact)
        inner = (back * bends[index]).astype(jnp.bfloat16)
        inners.append(inner)
        upstream = upstream + jnp.einsum("rh,dh->rd", inner, adaptor_in[index], **exact)
        if index == 1:
            pairs = [(slopes[k], lifteds[k : k + 1]) for k in range(2)]
            of_heads = begin(product(pairs, groups, group))
            slopes[2][0], arrived = pin(slopes[2][0], of_heads[1])
            of_heads = advance(arrive(of_heads, arrived))
    upstream = upstream.reshape(members, block, -1)
    came = [swap(upstream[j].astype(jnp.bfloat16), "mp", j) for j in range(1, members)]

    mine, *inners = pin(upstream[0], *inners)
    of_rest = begin(
        product([([final], inners), (slopes[2], lifteds[2:])], groups, group, 2**35)
    )
    came[0], one, two = pin(came[0], of_heads[1], of_rest[1])
    of_heads = arrive(of_heads, one)
    of_rest = advance(arrive(of_rest, two))
    total = mine
    for piece in came:
        total = total + piece.astype(jnp.float32)
    through_rows = normalize_back(total, final_gain, normal_rows, inverse_rows)
    through_rows = through_rows.astype(jnp.bfloat16)
    came = [swap(through_rows, "mp", j) for j in range(1, members)]
    turned = through_rows.T.reshape(groups, -1, block)
    turned = [lax.dynamic_index_in_dim(turned, group ^ o, 0) for o in range(groups)]
    odd = swap(jnp.concatenate(turned[1::2], axis=0), "dp", 1)
    came[-1], odd, one, two, actives = pin(came[-1], odd, of_heads[1], of_rest[1], actives)
    of_heads, of_rest = arrive(of_heads, one), arrive(of_rest, two)
    through = jnp.concatenate([through_rows, *came], axis=0)
    both = [jnp.concatenate([turned[2 * o], odd[o : o + 1]]) for o in range(groups // 2)]
    both = [both[0]] + [swap(both[o], "dp", 2 * o) for o in range(1, groups // 2)]

    back_two = jnp.einsum("rd,fd->rf", through, narrow_weight, **exact)
    inner_two = (back_two * bend_two).astype(jnp.bfloat16)
    inner_two, one, two = pin(inner_two, of_heads[1], of_rest[1])
    of_heads, of_rest = settle(arrive(of_heads, one)), settle(arrive(of_rest, two))
    of_widen = begin(product([([first], [inner_two])], groups, group, 2**35))
    of_widen = advance(of_widen, True)
    keep, *both = pin(of_widen[0], *both)
    of_widen = (keep, *of_widen[1:])
    columns = jnp.concatenate(both, axis=0)
    columns = [columns] + [swap(columns, "mp", j) for j in range(1, members)]
    of_heads, of_rest = settle(of_heads), settle(of_rest)
    while of_widen[2]:
        one, two, *columns[1:] = pin(of_widen[1], of_rest[1], *columns[1:])
        of_widen, of_rest = arrive(of_widen, one), arrive(of_rest, two)
        of_widen = advance(of_widen, True)
    wide = lifteds[0].shape[1]
    cuts = [head.shape[1] // groups for head in heads]
    deep = final.shape[1] // groups
    spans = [(k * wide, (k + 1) * wide) for k in range(4)]
    made = finish(
        [of_heads, of_rest],
        [
            [(cuts[0], *spans[0]), (cuts[1], *spans[1])],
            [(deep, *span) for span in spans[:3]] + [(cuts[2], *spans[3])],
        ],
    )
    head_grads = [made[0].T, made[1].T, made[5].T]
    grad_adaptor = jnp.stack(made[2:5])
    grad_narrow = narrow_sum(group, actives, columns).T
    keep, came, _ = of_widen
    came, grad_narrow, grad_adaptor, *head_grads = pin(
        came, grad_narrow, grad_adaptor, *head_grads
    )
    grad_widen = (keep[0].astype(jnp.float32) + came[0].astype(jnp.float32)).T
    return (grad_widen, grad_narrow, grad_adaptor, *head_grads)


def solution(mesh):
    placed = (
        P("dp", None),
        P(),
        P(None, "mp"),
        P("mp", None),
        P(),
        P(None, None, "mp"),
        P("mp", None),
        P("mp", None),
        P("mp", None),
        P(None, "dp", "mp"),
        P(None, "dp", "mp"),
        P(None, "dp", "mp"),
        P(),
        P(),
    )
    return jax.shard_map(
        local,
        mesh=mesh,
        in_specs=placed,
        out_specs=(
            P("mp", "dp"),
            P("mp", "dp"),
            P(None, "dp", "mp"),
            P("mp", "dp"),
            P("mp", "dp"),
            P("mp", "dp"),
        ),
        check_vma=False,
    )
```
